32 devices in a mesh: group: 2 (over y), seq: 4 (over z), head: 2 (over x), tp: 2 (over core).
Axes of the slice: x: 2, y: 2, z: 4, core: 2. Of those that a mesh axis runs over, the one named last changes fastest.
Arguments:
- query_field: bfloat16 [2, 1024, 2048], P(None, ('group', 'seq', 'head'), 'tp'), parts along dimension 1, may hold values from -21 to 21
- key_field: bfloat16 [2, 1024, 2048], P(None, ('group', 'seq', 'head'), 'tp'), parts along dimension 1, may hold values from -21 to 21
- value_field: bfloat16 [2, 1024, 2048], P(None, ('group', 'seq', 'head'), 'tp'), parts along dimension 1, may hold values from -21 to 21
- positions: int32 [1024], P(('group', 'seq', 'head')), parts along dimension 0, may hold values from 0 to 511, each once
- timesteps: int32 [4], P('group'), parts along dimension 0, may hold values from 0 to 999
- w_out: bfloat16 [2048, 3072], P('tp'), may hold values from -0.75 to 0.75
- w_time: bfloat16 [256, 3072], P(None, 'tp'), may hold values from -0.375 to 0.375
Outputs:
- gated_out: bfloat16 [2, 1024, 3072], P(None, ('group', 'seq', 'head'), 'tp'), parts along dimension 1
The draws below stay inside these ranges and needn't reach their ends.
There are 2 independent parts, one for each index of `group`. The reference program is written for one: setup_inputs(seed, part) draws one part's arguments, and reference() takes and returns one part's arrays. A program takes and returns all parts, laid end to end along the dimension named above; an argument that names none is the same for every part. Nothing has to cross between parts.
All inputs are finite; a program needn't handle non-finite values.
Results may differ from the reference program's by a relative error of at most 0.012.
Values may be sent and summed in bfloat16 or wider, within the bound.
A program may use at most 128 MiB of HBM per device.

```python
import math
import jax
import jax.numpy as jnp
from jax import lax

D = 3072
HEADS = 16
HD = 128
TIME_DIM = 256
LAT_H = 45
LAT_W = 80
STEPS = 2
TOKENS = 512


def stepped(start_field, drift_key, steady):
    changes = 0.6 * jax.random.normal(drift_key, (STEPS,) + start_field.shape, jnp.float32)
    changes = jnp.where(steady[None, :, None], 0.0, changes)
    step_mask = (jnp.arange(STEPS) > 0).astype(jnp.float32)[:, None, None]
    return jnp.clip(start_field[None] + step_mask * changes, -21.0, 21.0).astype(jnp.bfloat16)


def draw_query_field(key, part):
    key = jax.random.fold_in(key, 3)
    first_key, drift_key = jax.random.split(key, 2)
    field_shape = (TOKENS, HEADS * HD)
    start_field = 1.5 * jax.random.normal(first_key, field_shape, jnp.float32)
    steady = jnp.zeros((TOKENS,), dtype=bool)
    return stepped(start_field, drift_key, steady)


def draw_key_field(key, part):
    key = jax.random.fold_in(key, 7)
    first_key, drift_key = jax.random.split(key, 2)
    field_shape = (TOKENS, HEADS * HD)
    start_field = 1.5 * jax.random.normal(first_key, field_shape, jnp.float32)
    steady = jnp.zeros((TOKENS,), dtype=bool)
    return stepped(start_field, drift_key, steady)


def draw_value_field(key, part):
    key = jax.random.fold_in(key, 11)
    first_key, drift_key = jax.random.split(key, 2)
    field_shape = (TOKENS, HEADS * HD)
    start_field = jax.random.normal(first_key, field_shape, jnp.float32)
    steady = jnp.zeros((TOKENS,), dtype=bool)
    return stepped(start_field, drift_key, steady)


def steps_of(own_key, dims, cuts, least, top_value):
    def one(axis_at, blocks):
        draws = jax.random.uniform(jax.random.fold_in(jax.random.fold_in(own_key, 6), axis_at), (blocks,), jnp.float32, least / len(cuts), top_value / len(cuts))
        return jnp.repeat(jnp.exp(draws), dims[axis_at] // blocks).reshape((-1,) + (1,) * (len(dims) - axis_at - 1))

    factor_of = one(*cuts[0])
    for cut in cuts[1:]:
        factor_of = factor_of * one(*cut)
    return factor_of


def gaussian(own_key, shape, spread, most, cuts=(), kind=jnp.bfloat16):
    loudness = steps_of(own_key, shape, cuts, -0.22, 0.18) if cuts else 1.0
    entries = jax.random.normal(own_key, shape, jnp.float32) * spread * loudness
    return jnp.minimum(jnp.maximum(entries, -most), most).astype(kind)


def setup_inputs(seed: int = 0, part: int = 0) -> dict:
    keys = jax.random.split(jax.random.key(seed), 8)
    own_keys = jax.random.split(jax.random.fold_in(keys[7], part), 8)
    query_field = draw_query_field(jax.random.fold_in(jax.random.fold_in(keys[7], part), 71), part)
    key_field = draw_key_field(jax.random.fold_in(jax.random.fold_in(keys[7], part), 71), part)
    value_field = draw_value_field(jax.random.fold_in(jax.random.fold_in(keys[7], part), 71), part)
    positions = jax.random.permutation(own_keys[3], TOKENS).astype(jnp.int32)
    timesteps = jax.random.randint(own_keys[4], (STEPS,), 0, 1000).astype(jnp.int32)
    w_out = gaussian(keys[5], (HEADS * HD, D), (HEADS * HD // 32) ** -0.5, 0.75, ((0, 2),))
    w_time = gaussian(keys[6], (TIME_DIM, D), TIME_DIM ** -0.5, 0.375, ((1, 2),))
    return dict(query_field=query_field, key_field=key_field, value_field=value_field, positions=positions, timesteps=timesteps, w_out=w_out, w_time=w_time)


rope_theta = 256.0
time_base = 10000.0

def band_angles(positions):
    plane_size = LAT_H * LAT_W
    frame_index = positions // plane_size
    row_index = positions // LAT_W % LAT_H
    column_index = positions % LAT_W
    frame_band = HD // 8
    side_band = (HD - frame_band) // 2
    pieces = []
    for coordinate, band_width in ((frame_index, frame_band), (row_index, side_band), (column_index, side_band)):
        pair_index = jnp.arange(band_width // 2, dtype=jnp.float32)
        frequency = rope_theta ** (-2.0 * pair_index / band_width)
        pieces.append(coordinate.astype(jnp.float32)[:, None] * frequency[None, :])
    return jnp.concatenate(pieces, axis=1)

def rotate(block_rows, cosine, sine_table):
    row_count = block_rows.shape[0]
    paired = block_rows.astype(jnp.float32).reshape(row_count, -1, HD // 2, 2)
    leading = paired[..., 0]
    second = paired[..., 1]
    cos_part = cosine[:, None, :]
    sin_part = sine_table[:, None, :]
    turned = jnp.stack([leading * cos_part - second * sin_part, leading * sin_part + second * cos_part], axis=-1)
    return turned.reshape(row_count, -1).astype(jnp.bfloat16)

def encode(fresh, base_rows):
    row_count = fresh.shape[0]
    residual = (fresh.astype(jnp.float32) - base_rows.astype(jnp.float32)).reshape(row_count, -1, HD)
    largest = lax.optimization_barrier(jnp.max(jnp.abs(residual), axis=2))
    code_scale = lax.optimization_barrier(((largest + 1e-06) / 120.0).astype(jnp.bfloat16))
    code_values = jnp.floor(residual / code_scale.astype(jnp.float32)[:, :, None] + 0.5)
    return (code_values.reshape(row_count, -1).astype(jnp.bfloat16), code_scale)

def decode_residual(code_values, code_scale, base_rows):
    row_count = code_values.shape[0]
    shaped = code_values.astype(jnp.float32).reshape(row_count, -1, HD) * code_scale.astype(jnp.float32)[:, :, None]
    return (base_rows.astype(jnp.float32) + shaped.reshape(row_count, -1)).astype(jnp.bfloat16)

def time_gate(step_value, w_time):
    half_feature_width = w_time.shape[0] // 2
    pair_index = jnp.arange(half_feature_width, dtype=jnp.float32)
    frequency = jnp.exp(-math.log(time_base) * pair_index / half_feature_width)
    phases = step_value.astype(jnp.float32) * frequency
    embedding = jnp.concatenate([jnp.cos(phases), jnp.sin(phases)])
    return lax.optimization_barrier(jnp.sum(embedding[:, None] * w_time.astype(jnp.float32), axis=0))

def attend_heads(rotated_q, used_keys, used_values):
    token_count = rotated_q.shape[0]
    query_block = math.gcd(token_count, 1024)
    score_scale = 1.0 / math.sqrt(HD)

    def split_heads(matrix):
        return matrix.reshape(token_count, HEADS, HD).transpose(1, 0, 2)

    def one_head(head_arrays):
        head_queries, head_keys, head_values = head_arrays
        blocks = head_queries.reshape(token_count // query_block, query_block, HD)

        def one_block(block_queries):
            scores = jnp.dot(block_queries, head_keys.T, preferred_element_type=jnp.float32) * score_scale
            row_max = lax.optimization_barrier(jnp.max(scores, axis=1, keepdims=True))
            exponent = jnp.exp(scores - row_max)
            row_sum = lax.optimization_barrier(jnp.sum(exponent, axis=1, keepdims=True))
            mixed = jnp.dot(exponent.astype(jnp.bfloat16), head_values, preferred_element_type=jnp.float32)
            return (mixed / row_sum).astype(jnp.bfloat16)
        return lax.map(one_block, blocks).reshape(token_count, HD)
    per_head = lax.map(one_head, (split_heads(rotated_q), split_heads(used_keys), split_heads(used_values)))
    return per_head.transpose(1, 0, 2).reshape(token_count, HEADS * HD)

def reference(query_field, key_field, value_field, positions, timesteps, w_out, w_time):
    angles = band_angles(positions)
    cosine = jnp.cos(angles)
    sine_table = jnp.sin(angles)
    results = []
    used_keys = None
    used_values = None
    for step_index in range(STEPS):
        rotated_q = rotate(query_field[step_index], cosine, sine_table)
        rotated_k = rotate(key_field[step_index], cosine, sine_table)
        if step_index == 0:
            used_keys = rotated_k
            used_values = value_field[0]
        else:
            key_codes, key_scale = encode(rotated_k, used_keys)
            value_codes, value_scale = encode(value_field[step_index], used_values)
            used_keys = decode_residual(key_codes, key_scale, used_keys)
            used_values = decode_residual(value_codes, value_scale, used_values)
        attended = attend_heads(rotated_q, used_keys, used_values)
        projected = jnp.dot(attended, w_out, preferred_element_type=jnp.float32)
        gate_values = time_gate(timesteps[step_index], w_time)
        results.append((projected * gate_values[None, :]).astype(jnp.bfloat16))
    return jnp.stack(results)
```

```python
import math

import jax
import jax.numpy as jnp
import numpy as np
from jax import lax
from jax.experimental import pallas as pl
from jax.experimental.pallas import tpu as pltpu
from jax.sharding import PartitionSpec as P

HD = 128
LAT_H = 45
LAT_W = 80
STEPS = 2


rope_theta = 256.0
time_base = 10000.0
lowest = -1e30


def band_angles(positions):
    plane_size = LAT_H * LAT_W
    frame_index = positions // plane_size
    row_index = positions // LAT_W % LAT_H
    column_index = positions % LAT_W
    frame_band = HD // 8
    side_band = (HD - frame_band) // 2
    pieces = []
    for coordinate, band_width in (
        (frame_index, frame_band),
        (row_index, side_band),
        (column_index, side_band),
    ):
        pair_index = jnp.arange(band_width // 2, dtype=jnp.float32)
        frequency = rope_theta ** (-2.0 * pair_index / band_width)
        pieces.append(coordinate.astype(jnp.float32)[:, None] * frequency[None, :])
    return jnp.concatenate(pieces, axis=1)


def rotate(block_rows, cosine, sine_table):
    row_count = block_rows.shape[0]
    paired = block_rows.astype(jnp.float32).reshape(row_count, -1, HD // 2, 2)
    leading = paired[..., 0]
    second = paired[..., 1]
    cos_part = cosine[:, None, :]
    sin_part = sine_table[:, None, :]
    turned = jnp.stack(
        [leading * cos_part - second * sin_part, leading * sin_part + second * cos_part], axis=-1
    )
    return turned.reshape(row_count, -1).astype(jnp.bfloat16)


def encode(fresh, base_rows):
    row_count = fresh.shape[0]
    residual = (fresh.astype(jnp.float32) - base_rows.astype(jnp.float32)).reshape(
        row_count, -1, HD
    )
    largest = jnp.max(jnp.abs(residual), axis=2)
    code_scale = lax.optimization_barrier(((largest + 1e-06) / 120.0).astype(jnp.bfloat16))
    code_values = jnp.floor(residual / code_scale.astype(jnp.float32)[:, :, None] + 0.5)
    return (code_values.reshape(row_count, -1).astype(jnp.bfloat16), code_scale)


def decode_residual(code_values, code_scale, base_rows):
    row_count = code_values.shape[0]
    shaped = (
        code_values.astype(jnp.float32).reshape(row_count, -1, HD)
        * code_scale.astype(jnp.float32)[:, :, None]
    )
    return (base_rows.astype(jnp.float32) + shaped.reshape(row_count, -1)).astype(jnp.bfloat16)


def time_gate(step_value, w_time):
    half_feature_width = w_time.shape[0] // 2
    pair_index = jnp.arange(half_feature_width, dtype=jnp.float32)
    frequency = jnp.exp(-math.log(time_base) * pair_index / half_feature_width)
    phases = step_value.astype(jnp.float32) * frequency
    embedding = jnp.concatenate([jnp.cos(phases), jnp.sin(phases)])
    return jnp.sum(embedding[:, None] * w_time.astype(jnp.float32), axis=0)


def fold_update(fold_state, query_rows, key_piece, value_piece):
    running_max, running_sum, weighted = fold_state
    head_count = running_max.shape[0]
    score_scale = 1.0 / math.sqrt(HD)
    new_max, new_sum, new_weighted = ([], [], [])
    for head_index in range(head_count):
        lower = head_index * HD
        head_queries = query_rows[:, lower : lower + HD]
        head_keys = key_piece[:, lower : lower + HD]
        head_values = value_piece[:, lower : lower + HD]
        scores = (
            jnp.dot(head_queries, head_keys.T, preferred_element_type=jnp.float32) * score_scale
        )
        top_now = jnp.maximum(running_max[head_index], jnp.max(scores, axis=1))
        exponent = jnp.exp(scores - top_now[:, None])
        rescale = jnp.exp(running_max[head_index] - top_now)
        new_sum.append(running_sum[head_index] * rescale + jnp.sum(exponent, axis=1))
        mixed = jnp.dot(
            exponent.astype(jnp.bfloat16), head_values, preferred_element_type=jnp.float32
        )
        new_weighted.append(weighted[head_index] * rescale[:, None] + mixed)
        new_max.append(top_now)
    return (jnp.stack(new_max), jnp.stack(new_sum), jnp.stack(new_weighted))


def body(query_field, key_field, value_field, positions, timesteps, w_out, w_time):
    angles = band_angles(positions)
    cosine = jnp.cos(angles)
    sine_table = jnp.sin(angles)
    results = []
    own_keys = None
    own_values = None
    anchor_key_rows = None
    base_values = None
    for step_index in range(STEPS):
        rotated_q = rotate(query_field[step_index], cosine, sine_table)
        rotated_k = rotate(key_field[step_index], cosine, sine_table)
        fresh_values = value_field[step_index]
        query_rows, key_rows, value_rows = (
            lax.all_to_all(rotated_q, "head", split_axis=1, concat_axis=0, tiled=True),
            lax.all_to_all(rotated_k, "head", split_axis=1, concat_axis=0, tiled=True),
            lax.all_to_all(fresh_values, "head", split_axis=1, concat_axis=0, tiled=True),
        )
        head_count = query_rows.shape[1] // HD
        query_count = query_rows.shape[0]
        start_state = (
            jnp.full((head_count, query_count), lowest, jnp.float32),
            jnp.zeros((head_count, query_count), jnp.float32),
            jnp.zeros((head_count, query_count, HD), jnp.float32),
        )
        if step_index > 0:
            key_codes, key_scale = encode(key_rows, own_keys)
            value_codes, value_scale = encode(value_rows, own_values)
            own_keys = decode_residual(key_codes, key_scale, own_keys)
            own_values = decode_residual(value_codes, value_scale, own_values)
        if step_index == 0:
            anchor_key_rows, base_values = (
                lax.all_gather(key_rows, "seq", axis=0, tiled=True),
                lax.all_gather(value_rows, "seq", axis=0, tiled=True),
            )
            fold_state = fold_update(start_state, query_rows, anchor_key_rows, base_values)
        else:
            all_key_codes, all_value_codes, all_key_scales, all_value_scales = (
                lax.all_gather(key_codes, "seq", axis=0, tiled=True),
                lax.all_gather(value_codes, "seq", axis=0, tiled=True),
                lax.all_gather(key_scale, "seq", axis=0, tiled=True),
                lax.all_gather(value_scale, "seq", axis=0, tiled=True),
            )
            anchor_key_rows = decode_residual(all_key_codes, all_key_scales, anchor_key_rows)
            base_values = decode_residual(all_value_codes, all_value_scales, base_values)
            fold_state = fold_update(start_state, query_rows, anchor_key_rows, base_values)
        if step_index == 0:
            own_keys = key_rows
            own_values = value_rows
        running_max, running_sum, weighted = fold_state
        attended = (weighted / running_sum[:, :, None]).astype(jnp.bfloat16)
        attended = attended.transpose(1, 0, 2).reshape(query_count, head_count * HD)
        token_rows = lax.all_to_all(attended, "head", split_axis=0, concat_axis=1, tiled=True)
        partial_terms = jnp.dot(token_rows, w_out, preferred_element_type=jnp.float32)
        projected = lax.psum_scatter(partial_terms, "tp", scatter_dimension=1, tiled=True)
        gate_values = time_gate(timesteps[step_index], w_time)
        results.append((projected * gate_values[None, :]).astype(jnp.bfloat16))
    return jnp.stack(results)


MESH = pl.DeviceIdType.MESH


def feature_table():
    frame_band = HD // 8
    side_band = (HD - frame_band) // 2
    rope = []
    for band_width in (frame_band, side_band, side_band):
        pair_index = np.arange(band_width // 2)
        rope.append(np.repeat(rope_theta ** (-2.0 * pair_index / band_width), 2))
    table = np.zeros((8, HD), np.float32)
    table[0] = np.concatenate(rope)
    return table


def time_table(half_width):
    index = np.arange(half_width)
    table = np.zeros((8, half_width), np.float32)
    table[0] = np.exp(-math.log(time_base) * index / half_width)
    return table


def flipped(index, mask):
    out = index
    bit = 1
    while bit <= mask:
        if mask & bit:
            out = out + bit * (1 - 2 * ((index // bit) % 2))
        bit *= 2
    return out


def fused_kernel(
    sizes,
    q_hbm,
    k_hbm,
    v_hbm,
    pos_hbm,
    time_hbm,
    w_out_hbm,
    w_time_hbm,
    rope_hbm,
    freq_hbm,
    out_hbm,
    q_in,
    k_in,
    v_in,
    pos_in,
    time_in,
    w_out,
    w_time,
    rope_in,
    freq_in,
    sent,
    got,
    att_out,
    att_in,
    part_out,
    part_in,
    part_own,
    out_buf,
    gate_buf,
    load_sem,
    out_sem,
    send_sem,
    recv_sem,
    att_send_sem,
    att_recv_sem,
    part_send_sem,
    part_recv_sem,
):
    n_seq, n_head, steps, tokens, half, chunk = sizes
    peers = n_seq * n_head
    chunks = half // chunk
    seq = lax.axis_index("seq")
    head = lax.axis_index("head")
    core = lax.axis_index("tp")
    me = seq * n_head + head

    loads = [
        pltpu.make_async_copy(source, target, load_sem.at[slot])
        for slot, (source, target) in enumerate(
            (
                (v_hbm, v_in),
                (pos_hbm, pos_in),
                (rope_hbm, rope_in),
                (k_hbm, k_in),
                (q_hbm, q_in),
                (time_hbm, time_in),
                (freq_hbm, freq_in),
                (w_time_hbm, w_time),
                (w_out_hbm, w_out),
            )
        )
    ]
    for load in loads:
        load.start()

    def place(mask):
        other = flipped(me, mask)
        return {"seq": other // n_head, "head": other % n_head}

    partner = {"tp": 1 - core}
    barrier = pltpu.get_barrier_semaphore()
    for mask in range(1, peers):
        pl.semaphore_signal(barrier, inc=1, device_id=place(mask), device_id_type=MESH)
    pl.semaphore_signal(barrier, inc=1, device_id=partner, device_id_type=MESH)

    order = list(range(peers - 1, -1, -1))

    def columns(mask):
        return pl.ds(pl.multiple_of(flipped(me, mask) * HD, HD), HD)

    def rows(mask):
        return pl.ds(mask * tokens, tokens)

    def send(step, kind, mask):
        if kind == 2 and step == 0:
            source = v_in.at[0, :, columns(mask)]
        else:
            source = sent.at[step, kind, rows(mask)]
        return pltpu.make_async_remote_copy(
            src_ref=source,
            dst_ref=got.at[step, kind, rows(mask)],
            send_sem=send_sem.at[step, kind, mask],
            recv_sem=recv_sem.at[step, kind, mask],
            device_id=place(mask),
            device_id_type=MESH,
        )

    def emit(step, kind, mask, block):
        if mask == 0:
            got[step, kind, rows(0)] = block
        else:
            sent[step, kind, rows(mask)] = block
            send(step, kind, mask).start()

    loads[1].wait()
    loads[2].wait()
    place_row = pos_in[...].astype(jnp.float32)
    square = (tokens, tokens)
    diagonal = lax.broadcasted_iota(jnp.int32, square, 0) == lax.broadcasted_iota(
        jnp.int32, square, 1
    )
    place_column = jnp.sum(
        jnp.where(diagonal, jnp.broadcast_to(place_row, square), 0.0), axis=1, keepdims=True
    )
    plane = float(LAT_H * LAT_W)
    line = jnp.floor((place_column + 0.5) * (1.0 / LAT_W))
    frame_index = jnp.floor((place_column + 0.5) * (1.0 / plane))
    row_index = line - frame_index * LAT_H
    column_index = place_column - line * LAT_W
    lane = lax.broadcasted_iota(jnp.int32, (tokens, HD), 1)
    frame_band = HD // 8
    side_band = (HD - frame_band) // 2
    coordinate = jnp.where(
        lane < frame_band,
        frame_index,
        jnp.where(lane < frame_band + side_band, row_index, column_index),
    )
    angles = coordinate * rope_in[0:1, :]
    cosine = jnp.cos(angles)
    even = lane % 2 == 0
    sine = jnp.where(even, -jnp.sin(angles), jnp.sin(angles))

    def turned(block):
        wide = block.astype(jnp.float32)
        swapped = jnp.where(even, pltpu.roll(wide, HD - 1, 1), pltpu.roll(wide, 1, 1))
        return (wide * cosine + swapped * sine).astype(jnp.bfloat16)

    def recoded(fresh, base):
        wide_base = base.astype(jnp.float32)
        residual = fresh.astype(jnp.float32) - wide_base
        largest = jnp.max(jnp.abs(residual), axis=1, keepdims=True)
        scale = ((largest + 1e-06) / 120.0).astype(jnp.bfloat16).astype(jnp.float32)
        code = jnp.floor(residual / scale + 0.5)
        return (wide_base + code * scale).astype(jnp.bfloat16)

    loads[0].wait()
    pl.semaphore_wait(barrier, peers)
    for mask in order:
        if mask == 0:
            got[0, 2, rows(0)] = v_in[0, :, columns(0)]
        else:
            send(0, 2, mask).start()
    loads[3].wait()
    for mask in order:
        emit(0, 1, mask, turned(k_in[0, :, columns(mask)]))
    loads[4].wait()
    for mask in order:
        emit(0, 0, mask, turned(q_in[0, :, columns(mask)]))
    for step in range(1, steps):
        for mask in order:
            base = v_in[0, :, columns(mask)] if step == 1 else v_in[step - 1, :, columns(mask)]
            block = recoded(v_in[step, :, columns(mask)], base)
            if step + 1 < steps:
                v_in[step, :, columns(mask)] = block
            emit(step, 2, mask, block)
        for mask in order:
            kept = got if mask == 0 else sent
            base = kept[step - 1, 1, rows(mask)]
            emit(step, 1, mask, recoded(turned(k_in[step, :, columns(mask)]), base))
        for mask in order:
            emit(step, 0, mask, turned(q_in[step, :, columns(mask)]))

    for load in loads[5:8]:
        load.wait()
    half_width = freq_in.shape[1]
    for step in range(steps):
        phases = time_in[0:1, step : step + 1].astype(jnp.float32) * freq_in[0:1, :]
        total = jnp.zeros((8, half), jnp.float32)
        for lower, wave in ((0, jnp.cos(phases)), (half_width, jnp.sin(phases))):
            first = wave.astype(jnp.bfloat16)
            rest = wave - first.astype(jnp.float32)
            second = rest.astype(jnp.bfloat16)
            third = (rest - second.astype(jnp.float32)).astype(jnp.bfloat16)
            which = lax.broadcasted_iota(jnp.int32, (8, half_width), 0)
            stacked = jnp.where(
                which == 0,
                first.astype(jnp.float32),
                jnp.where(
                    which == 1,
                    second.astype(jnp.float32),
                    jnp.where(which == 2, third.astype(jnp.float32), 0.0),
                ),
            ).astype(jnp.bfloat16)
            total = total + jnp.dot(
                stacked, w_time[lower : lower + half_width, :], preferred_element_type=jnp.float32
            )
        gate_buf[step] = jnp.broadcast_to(jnp.sum(total, axis=0, keepdims=True), (8, half))

    def give_back(step, mask):
        return pltpu.make_async_remote_copy(
            src_ref=att_out.at[step, rows(mask)],
            dst_ref=att_in.at[step, :, columns(0)],
            send_sem=att_send_sem.at[step, mask],
            recv_sem=att_recv_sem.at[step, mask],
            device_id=place(mask),
            device_id_type=MESH,
        )

    score_scale = 1.0 / math.sqrt(HD)

    def attend(step):
        for kind in (2, 1, 0):
            for mask in range(1, peers):
                send(step, kind, mask).wait_recv()
        keys = got[step, 1]
        values = got[step, 2]
        group = 2 if peers % 2 == 0 else 1
        for start in range(peers - group, -1, -group):
            queries = got[step, 0, start * tokens : (start + group) * tokens]
            scores = (
                lax.dot_general(
                    queries, keys, (((1,), (1,)), ((), ())), preferred_element_type=jnp.float32
                )
                * score_scale
            )
            weights = jnp.exp(scores - jnp.max(scores, axis=1, keepdims=True))
            totals = jnp.sum(weights, axis=1, keepdims=True)
            mixed = jnp.dot(
                weights.astype(jnp.bfloat16), values, preferred_element_type=jnp.float32
            )
            attended = (mixed / totals).astype(jnp.bfloat16)
            for mask in range(start + group - 1, start - 1, -1):
                block = attended[(mask - start) * tokens : (mask - start + 1) * tokens]
                if mask == 0:
                    att_in[step, :, columns(0)] = block
                else:
                    att_out[step, rows(mask)] = block
                    give_back(step, mask).start()

    def share(step, piece):
        return pltpu.make_async_remote_copy(
            src_ref=part_out.at[step, piece],
            dst_ref=part_in.at[step, piece],
            send_sem=part_send_sem.at[step, piece],
            recv_sem=part_recv_sem.at[step, piece],
            device_id=partner,
            device_id_type=MESH,
        )

    def project(step):
        for mask in range(1, peers):
            pltpu.make_async_remote_copy(
                src_ref=att_out.at[step, rows(mask)],
                dst_ref=att_in.at[step, :, columns(mask)],
                send_sem=att_send_sem.at[step, mask],
                recv_sem=att_recv_sem.at[step, mask],
                device_id=place(mask),
                device_id_type=MESH,
            ).wait_recv()
        if step == 0:
            loads[8].wait()
        attended = att_in[step]
        for piece in range(chunks):
            lower = pl.multiple_of((1 - core) * half + piece * chunk, HD)
            part_out[step, piece] = jnp.dot(
                attended, w_out[:, pl.ds(lower, chunk)], preferred_element_type=jnp.float32
            )
            share(step, piece).start()
        for piece in range(chunks):
            lower = pl.multiple_of(core * half + piece * chunk, HD)
            part_own[step, piece] = jnp.dot(
                attended, w_out[:, pl.ds(lower, chunk)], preferred_element_type=jnp.float32
            )

    def finish(step):
        for piece in range(chunks):
            share(step, piece).wait_recv()
            cut = slice(piece * chunk, (piece + 1) * chunk)
            projected = part_own[step, piece] + part_in[step, piece]
            out_buf[step, :, cut] = (projected * gate_buf[step, 0:1, cut]).astype(jnp.bfloat16)
        copy = pltpu.make_async_copy(out_buf.at[step], out_hbm.at[step], out_sem.at[step])
        copy.start()
        return copy

    for step in range(steps):
        attend(step)
    copies = []
    for step in range(steps):
        project(step)
        if step > 0:
            copies.append(finish(step - 1))
    copies.append(finish(steps - 1))

    for step in range(steps):
        for mask in range(1, peers):
            for kind in range(3):
                send(step, kind, mask).wait_send()
            give_back(step, mask).wait_send()
        for piece in range(chunks):
            share(step, piece).wait_send()
    for copy in copies:
        copy.wait()


def fused_body(n_seq, n_head, query_field, key_field, value_field, positions, timesteps, w_out, w_time):
    steps, tokens, features = query_field.shape
    half = w_time.shape[1]
    peers = n_seq * n_head
    chunk = 512 if half % 512 == 0 else HD
    chunks = half // chunk
    bf16, f32 = jnp.bfloat16, jnp.float32
    dma = pltpu.SemaphoreType.DMA
    rope = jnp.asarray(feature_table())
    freq = jnp.asarray(time_table(w_time.shape[0] // 2))
    sizes = (n_seq, n_head, steps, tokens, half, chunk)
    scratch = [
        pltpu.VMEM(query_field.shape, bf16),
        pltpu.VMEM(key_field.shape, bf16),
        pltpu.VMEM(value_field.shape, bf16),
        pltpu.VMEM((1, tokens), jnp.int32),
        pltpu.VMEM((1, steps), jnp.int32),
        pltpu.VMEM(w_out.shape, bf16),
        pltpu.VMEM(w_time.shape, bf16),
        pltpu.VMEM(rope.shape, f32),
        pltpu.VMEM(freq.shape, f32),
        pltpu.VMEM((steps, 3, peers * tokens, HD), bf16),
        pltpu.VMEM((steps, 3, peers * tokens, HD), bf16),
        pltpu.VMEM((steps, peers * tokens, HD), bf16),
        pltpu.VMEM((steps, tokens, features), bf16),
        pltpu.VMEM((steps, chunks, tokens, chunk), f32),
        pltpu.VMEM((steps, chunks, tokens, chunk), f32),
        pltpu.VMEM((steps, chunks, tokens, chunk), f32),
        pltpu.VMEM((steps, tokens, half), bf16),
        pltpu.VMEM((steps, 8, half), f32),
        dma((9,)),
        dma((steps,)),
        dma((steps, 3, peers)),
        dma((steps, 3, peers)),
        dma((steps, peers)),
        dma((steps, peers)),
        dma((steps, chunks)),
        dma((steps, chunks)),
    ]
    return pl.pallas_call(
        lambda *refs: fused_kernel(sizes, *refs),
        out_shape=jax.ShapeDtypeStruct((steps, tokens, half), bf16),
        in_specs=[pl.BlockSpec(memory_space=pl.ANY)] * 9,
        out_specs=pl.BlockSpec(memory_space=pl.ANY),
        scratch_shapes=scratch,
        compiler_params=pltpu.CompilerParams(
            collective_id=0, has_side_effects=True, vmem_limit_bytes=40 * 1024 * 1024
        ),
    )(
        query_field,
        key_field,
        value_field,
        positions.reshape(1, tokens),
        timesteps.reshape(1, steps),
        w_out,
        w_time,
        rope,
        freq,
    )


def solution(mesh):
    placed = (
        P(None, ("group", "seq", "head"), "tp"),
        P(None, ("group", "seq", "head"), "tp"),
        P(None, ("group", "seq", "head"), "tp"),
        P(("group", "seq", "head")),
        P("group"),
        P("tp", None),
        P(None, "tp"),
    )
    n_seq, n_head = mesh.shape["seq"], mesh.shape["head"]
    peers = n_seq * n_head

    def chosen(query_field, *rest):
        local_heads = query_field.shape[2] // HD
        tokens = query_field.shape[1]
        if (
            local_heads == peers
            and peers & (peers - 1) == 0
            and mesh.shape["tp"] == 2
            and tokens % 16 == 0
        ):
            return fused_body(n_seq, n_head, query_field, *rest)
        return body(query_field, *rest)

    return jax.shard_map(
        chosen,
        mesh=mesh,
        in_specs=placed,
        out_specs=P(None, ("group", "seq", "head"), "tp"),
        check_vma=False,
    )
```

```python
import math

import jax
import jax.numpy as jnp
import numpy as np
from jax import lax
from jax.experimental import pallas as pl
from jax.experimental.pallas import tpu as pltpu
from jax.sharding import PartitionSpec as P

HD = 128
LAT_H = 45
LAT_W = 80
STEPS = 2


rope_theta = 256.0
time_base = 10000.0
lowest = -1e30


def band_angles(positions):
    plane_size = LAT_H * LAT_W
    frame_index = positions // plane_size
    row_index = positions // LAT_W % LAT_H
    column_index = positions % LAT_W
    frame_band = HD // 8
    side_band = (HD - frame_band) // 2
    pieces = []
    for coordinate, band_width in (
        (frame_index, frame_band),
        (row_index, side_band),
        (column_index, side_band),
    ):
        pair_index = jnp.arange(band_width // 2, dtype=jnp.float32)
        frequency = rope_theta ** (-2.0 * pair_index / band_width)
        pieces.append(coordinate.astype(jnp.float32)[:, None] * frequency[None, :])
    return jnp.concatenate(pieces, axis=1)


def rotate(block_rows, cosine, sine_table):
    row_count = block_rows.shape[0]
    paired = block_rows.astype(jnp.float32).reshape(row_count, -1, HD // 2, 2)
    leading = paired[..., 0]
    second = paired[..., 1]
    cos_part = cosine[:, None, :]
    sin_part = sine_table[:, None, :]
    turned = jnp.stack(
        [leading * cos_part - second * sin_part, leading * sin_part + second * cos_part], axis=-1
    )
    return turned.reshape(row_count, -1).astype(jnp.bfloat16)


def encode(fresh, base_rows):
    row_count = fresh.shape[0]
    residual = (fresh.astype(jnp.float32) - base_rows.astype(jnp.float32)).reshape(
        row_count, -1, HD
    )
    largest = jnp.max(jnp.abs(residual), axis=2)
    code_scale = lax.optimization_barrier(((largest + 1e-06) / 120.0).astype(jnp.bfloat16))
    code_values = jnp.floor(residual / code_scale.astype(jnp.float32)[:, :, None] + 0.5)
    return (code_values.reshape(row_count, -1).astype(jnp.bfloat16), code_scale)


def decode_residual(code_values, code_scale, base_rows):
    row_count = code_values.shape[0]
    shaped = (
        code_values.astype(jnp.float32).reshape(row_count, -1, HD)
        * code_scale.astype(jnp.float32)[:, :, None]
    )
    return (base_rows.astype(jnp.float32) + shaped.reshape(row_count, -1)).astype(jnp.bfloat16)


def time_gate(step_value, w_time):
    half_feature_width = w_time.shape[0] // 2
    pair_index = jnp.arange(half_feature_width, dtype=jnp.float32)
    frequency = jnp.exp(-math.log(time_base) * pair_index / half_feature_width)
    phases = step_value.astype(jnp.float32) * frequency
    embedding = jnp.concatenate([jnp.cos(phases), jnp.sin(phases)])
    return jnp.sum(embedding[:, None] * w_time.astype(jnp.float32), axis=0)


def fold_update(fold_state, query_rows, key_piece, value_piece):
    running_max, running_sum, weighted = fold_state
    head_count = running_max.shape[0]
    score_scale = 1.0 / math.sqrt(HD)
    new_max, new_sum, new_weighted = ([], [], [])
    for head_index in range(head_count):
        lower = head_index * HD
        head_queries = query_rows[:, lower : lower + HD]
        head_keys = key_piece[:, lower : lower + HD]
        head_values = value_piece[:, lower : lower + HD]
        scores = (
            jnp.dot(head_queries, head_keys.T, preferred_element_type=jnp.float32) * score_scale
        )
        top_now = jnp.maximum(running_max[head_index], jnp.max(scores, axis=1))
        exponent = jnp.exp(scores - top_now[:, None])
        rescale = jnp.exp(running_max[head_index] - top_now)
        new_sum.append(running_sum[head_index] * rescale + jnp.sum(exponent, axis=1))
        mixed = jnp.dot(
            exponent.astype(jnp.bfloat16), head_values, preferred_element_type=jnp.float32
        )
        new_weighted.append(weighted[head_index] * rescale[:, None] + mixed)
        new_max.append(top_now)
    return (jnp.stack(new_max), jnp.stack(new_sum), jnp.stack(new_weighted))


def body(query_field, key_field, value_field, positions, timesteps, w_out, w_time):
    angles = band_angles(positions)
    cosine = jnp.cos(angles)
    sine_table = jnp.sin(angles)
    results = []
    own_keys = None
    own_values = None
    anchor_key_rows = None
    base_values = None
    for step_index in range(STEPS):
        rotated_q = rotate(query_field[step_index], cosine, sine_table)
        rotated_k = rotate(key_field[step_index], cosine, sine_table)
        fresh_values = value_field[step_index]
        query_rows, key_rows, value_rows = (
            lax.all_to_all(rotated_q, "head", split_axis=1, concat_axis=0, tiled=True),
            lax.all_to_all(rotated_k, "head", split_axis=1, concat_axis=0, tiled=True),
            lax.all_to_all(fresh_values, "head", split_axis=1, concat_axis=0, tiled=True),
        )
        head_count = query_rows.shape[1] // HD
        query_count = query_rows.shape[0]
        start_state = (
            jnp.full((head_count, query_count), lowest, jnp.float32),
            jnp.zeros((head_count, query_count), jnp.float32),
            jnp.zeros((head_count, query_count, HD), jnp.float32),
        )
        if step_index > 0:
            key_codes, key_scale = encode(key_rows, own_keys)
            value_codes, value_scale = encode(value_rows, own_values)
            own_keys = decode_residual(key_codes, key_scale, own_keys)
            own_values = decode_residual(value_codes, value_scale, own_values)
        if step_index == 0:
            anchor_key_rows, base_values = (
                lax.all_gather(key_rows, "seq", axis=0, tiled=True),
                lax.all_gather(value_rows, "seq", axis=0, tiled=True),
            )
            fold_state = fold_update(start_state, query_rows, anchor_key_rows, base_values)
        else:
            all_key_codes, all_value_codes, all_key_scales, all_value_scales = (
                lax.all_gather(key_codes, "seq", axis=0, tiled=True),
                lax.all_gather(value_codes, "seq", axis=0, tiled=True),
                lax.all_gather(key_scale, "seq", axis=0, tiled=True),
                lax.all_gather(value_scale, "seq", axis=0, tiled=True),
            )
            anchor_key_rows = decode_residual(all_key_codes, all_key_scales, anchor_key_rows)
            base_values = decode_residual(all_value_codes, all_value_scales, base_values)
            fold_state = fold_update(start_state, query_rows, anchor_key_rows, base_values)
        if step_index == 0:
            own_keys = key_rows
            own_values = value_rows
        running_max, running_sum, weighted = fold_state
        attended = (weighted / running_sum[:, :, None]).astype(jnp.bfloat16)
        attended = attended.transpose(1, 0, 2).reshape(query_count, head_count * HD)
        token_rows = lax.all_to_all(attended, "head", split_axis=0, concat_axis=1, tiled=True)
        partial_terms = jnp.dot(token_rows, w_out, preferred_element_type=jnp.float32)
        projected = lax.psum_scatter(partial_terms, "tp", scatter_dimension=1, tiled=True)
        gate_values = time_gate(timesteps[step_index], w_time)
        results.append((projected * gate_values[None, :]).astype(jnp.bfloat16))
    return jnp.stack(results)


MESH = pl.DeviceIdType.MESH


def feature_table():
    frame_band = HD // 8
    side_band = (HD - frame_band) // 2
    rope = []
    for band_width in (frame_band, side_band, side_band):
        pair_index = np.arange(band_width // 2)
        rope.append(np.repeat(rope_theta ** (-2.0 * pair_index / band_width), 2))
    table = np.zeros((8, HD), np.float32)
    table[0] = np.concatenate(rope)
    return table


def time_table(half_width):
    index = np.arange(half_width)
    table = np.zeros((8, half_width), np.float32)
    table[0] = np.exp(-math.log(time_base) * index / half_width)
    return table


def flipped(index, mask):
    out = index
    bit = 1
    while bit <= mask:
        if mask & bit:
            out = out + bit * (1 - 2 * ((index // bit) % 2))
        bit *= 2
    return out


def fused_kernel(
    sizes,
    q_hbm,
    k_hbm,
    v_hbm,
    pos_hbm,
    time_hbm,
    w_out_hbm,
    w_time_hbm,
    rope_hbm,
    freq_hbm,
    out_hbm,
    q_in,
    k_in,
    v_in,
    pos_in,
    time_in,
    w_out,
    w_time,
    rope_in,
    freq_in,
    sent,
    got,
    att_out,
    att_in,
    part_out,
    part_in,
    part_own,
    out_buf,
    gate_buf,
    load_sem,
    out_sem,
    send_sem,
    recv_sem,
    att_send_sem,
    att_recv_sem,
    part_send_sem,
    part_recv_sem,
):
    n_seq, n_head, steps, tokens, half, chunk = sizes
    peers = n_seq * n_head
    chunks = half // chunk
    seq = lax.axis_index("seq")
    head = lax.axis_index("head")
    core = lax.axis_index("tp")
    me = seq * n_head + head

    loads = [
        pltpu.make_async_copy(source, target, load_sem.at[slot])
        for slot, (source, target) in enumerate(
            (
                (v_hbm, v_in),
                (pos_hbm, pos_in),
                (rope_hbm, rope_in),
                (k_hbm, k_in),
                (q_hbm, q_in),
                (time_hbm, time_in),
                (freq_hbm, freq_in),
                (w_time_hbm, w_time),
                (w_out_hbm, w_out),
            )
        )
    ]
    for load in loads:
        load.start()

    def place(mask):
        other = flipped(me, mask)
        return {"seq": other // n_head, "head": other % n_head}

    partner = {"tp": 1 - core}
    barrier = pltpu.get_barrier_semaphore()
    for mask in range(1, peers):
        pl.semaphore_signal(barrier, inc=1, device_id=place(mask), device_id_type=MESH)
    pl.semaphore_signal(barrier, inc=1, device_id=partner, device_id_type=MESH)

    order = list(range(peers - 1, -1, -1))

    def columns(mask):
        return pl.ds(pl.multiple_of(flipped(me, mask) * HD, HD), HD)

    def rows(mask):
        return pl.ds(mask * tokens, tokens)

    def send(step, kind, mask):
        if kind == 2 and step == 0:
            source = v_in.at[0, :, columns(mask)]
        else:
            source = sent.at[step, kind, rows(mask)]
        return pltpu.make_async_remote_copy(
            src_ref=source,
            dst_ref=got.at[step, kind, rows(mask)],
            send_sem=send_sem.at[step, kind, mask],
            recv_sem=recv_sem.at[step, kind, mask],
            device_id=place(mask),
            device_id_type=MESH,
        )

    def emit(step, kind, mask, block):
        if mask == 0:
            got[step, kind, rows(0)] = block
        else:
            sent[step, kind, rows(mask)] = block
            send(step, kind, mask).start()

    loads[1].wait()
    loads[2].wait()
    place_row = pos_in[...].astype(jnp.float32)
    square = (tokens, tokens)
    diagonal = lax.broadcasted_iota(jnp.int32, square, 0) == lax.broadcasted_iota(
        jnp.int32, square, 1
    )
    place_column = jnp.sum(
        jnp.where(diagonal, jnp.broadcast_to(place_row, square), 0.0), axis=1, keepdims=True
    )
    plane = float(LAT_H * LAT_W)
    line = jnp.floor((place_column + 0.5) * (1.0 / LAT_W))
    frame_index = jnp.floor((place_column + 0.5) * (1.0 / plane))
    row_index = line - frame_index * LAT_H
    column_index = place_column - line * LAT_W
    lane = lax.broadcasted_iota(jnp.int32, (tokens, HD), 1)
    frame_band = HD // 8
    side_band = (HD - frame_band) // 2
    coordinate = jnp.where(
        lane < frame_band,
        frame_index,
        jnp.where(lane < frame_band + side_band, row_index, column_index),
    )
    angles = coordinate * rope_in[0:1, :]
    cosine = jnp.cos(angles)
    even = lane % 2 == 0
    sine = jnp.where(even, -jnp.sin(angles), jnp.sin(angles))

    def turned(block):
        wide = block.astype(jnp.float32)
        swapped = jnp.where(even, pltpu.roll(wide, HD - 1, 1), pltpu.roll(wide, 1, 1))
        return (wide * cosine + swapped * sine).astype(jnp.bfloat16)

    def recoded(fresh, base):
        wide_base = base.astype(jnp.float32)
        residual = fresh.astype(jnp.float32) - wide_base
        largest = jnp.max(jnp.abs(residual), axis=1, keepdims=True)
        scale = ((largest + 1e-06) / 120.0).astype(jnp.bfloat16).astype(jnp.float32)
        code = jnp.floor(residual / scale + 0.5)
        return (wide_base + code * scale).astype(jnp.bfloat16)

    loads[0].wait()
    pl.semaphore_wait(barrier, peers)
    far = order[: peers // 2]
    near = order[peers // 2 :]

    def emit_values(step, masks):
        for mask in masks:
            if step == 0 and mask == 0:
                got[0, 2, rows(0)] = v_in[0, :, columns(0)]
            elif step == 0:
                send(0, 2, mask).start()
            else:
                block = recoded(v_in[step, :, columns(mask)], v_in[step - 1, :, columns(mask)])
                if step + 1 < steps:
                    v_in[step, :, columns(mask)] = block
                emit(step, 2, mask, block)

    def emit_keys(step, masks):
        for mask in masks:
            block = turned(k_in[step, :, columns(mask)])
            if step > 0:
                kept = got if mask == 0 else sent
                block = recoded(block, kept[step - 1, 1, rows(mask)])
            emit(step, 1, mask, block)

    def emit_queries(step, masks):
        for mask in masks:
            emit(step, 0, mask, turned(q_in[step, :, columns(mask)]))

    emit_values(0, far)
    loads[3].wait()
    emit_keys(0, far)
    loads[4].wait()
    emit_queries(0, far)
    emit_values(0, near)
    emit_keys(0, near)
    emit_queries(0, near)
    for step in range(1, steps):
        emit_values(step, far)
        emit_keys(step, far)
        emit_values(step, near)
        emit_keys(step, near)
        emit_queries(step, near)
        emit_queries(step, far)

    for load in loads[5:8]:
        load.wait()
    half_width = freq_in.shape[1]
    for step in range(steps):
        phases = time_in[0:1, step : step + 1].astype(jnp.float32) * freq_in[0:1, :]
        total = jnp.zeros((8, half), jnp.float32)
        for lower, wave in ((0, jnp.cos(phases)), (half_width, jnp.sin(phases))):
            first = wave.astype(jnp.bfloat16)
            rest = wave - first.astype(jnp.float32)
            second = rest.astype(jnp.bfloat16)
            third = (rest - second.astype(jnp.float32)).astype(jnp.bfloat16)
            which = lax.broadcasted_iota(jnp.int32, (8, half_width), 0)
            stacked = jnp.where(
                which == 0,
                first.astype(jnp.float32),
                jnp.where(
                    which == 1,
                    second.astype(jnp.float32),
                    jnp.where(which == 2, third.astype(jnp.float32), 0.0),
                ),
            ).astype(jnp.bfloat16)
            total = total + jnp.dot(
                stacked, w_time[lower : lower + half_width, :], preferred_element_type=jnp.float32
            )
        gate_buf[step] = jnp.broadcast_to(jnp.sum(total, axis=0, keepdims=True), (8, half))

    def give_back(step, mask):
        return pltpu.make_async_remote_copy(
            src_ref=att_out.at[step, rows(mask)],
            dst_ref=att_in.at[step, :, columns(0)],
            send_sem=att_send_sem.at[step, mask],
            recv_sem=att_recv_sem.at[step, mask],
            device_id=place(mask),
            device_id_type=MESH,
        )

    score_scale = 1.0 / math.sqrt(HD)

    def attend(step):
        last = step == steps - 1
        for kind in (2, 1):
            for mask in range(1, peers):
                send(step, kind, mask).wait_recv()
        keys = got[step, 1]
        values = got[step, 2]
        for start in range(0, peers, 2):
            for mask in (start, start + 1):
                if mask > 0:
                    send(step, 0, mask).wait_recv()
            queries = got[step, 0, start * tokens : (start + 2) * tokens]
            scores = (
                lax.dot_general(
                    queries, keys, (((1,), (1,)), ((), ())), preferred_element_type=jnp.float32
                )
                * score_scale
            )
            weights = jnp.exp(scores - jnp.max(scores, axis=1, keepdims=True))
            totals = jnp.sum(weights, axis=1, keepdims=True)
            mixed = jnp.dot(
                weights.astype(jnp.bfloat16), values, preferred_element_type=jnp.float32
            )
            attended = (mixed / totals).astype(jnp.bfloat16)
            for mask in (start, start + 1):
                block = attended[(mask - start) * tokens : (mask - start + 1) * tokens]
                if mask == 0:
                    att_in[step, :, columns(0)] = block
                else:
                    att_out[step, rows(mask)] = block
                    if last or mask < peers // 2:
                        give_back(step, mask).start()
        if not last:
            for kind in (2, 1, 0):
                for mask in far:
                    send(step + 1, kind, mask).wait_send()
            for mask in far:
                give_back(step, mask).start()

    def share(step, piece):
        return pltpu.make_async_remote_copy(
            src_ref=part_out.at[step, piece],
            dst_ref=part_in.at[step, piece],
            send_sem=part_send_sem.at[step, piece],
            recv_sem=part_recv_sem.at[step, piece],
            device_id=partner,
            device_id_type=MESH,
        )

    def project(step):
        depth = att_in.shape[2] // 2
        side = seq // (n_seq // 2)
        if step == 0:
            loads[8].wait()
        for masks, block in ((range(1, peers // 2), side), (range(peers // 2, peers), 1 - side)):
            for mask in masks:
                pltpu.make_async_remote_copy(
                    src_ref=att_out.at[step, rows(mask)],
                    dst_ref=att_in.at[step, :, columns(mask)],
                    send_sem=att_send_sem.at[step, mask],
                    recv_sem=att_recv_sem.at[step, mask],
                    device_id=place(mask),
                    device_id_type=MESH,
                ).wait_recv()
            features = pl.ds(pl.multiple_of(block * depth, depth), depth)
            attended = att_in[step, :, features]
            first = masks[0] == 1
            for target, part in ((1 - core, part_out), (core, part_own)):
                for piece in range(chunks):
                    lower = pl.multiple_of(target * half + piece * chunk, HD)
                    term = jnp.dot(
                        attended,
                        w_out[features, pl.ds(lower, chunk)],
                        preferred_element_type=jnp.float32,
                    )
                    part[step, piece] = term if first else part[step, piece] + term
                    if part is part_out and not first:
                        share(step, piece).start()

    def finish(step):
        for piece in range(chunks):
            share(step, piece).wait_recv()
            cut = slice(piece * chunk, (piece + 1) * chunk)
            projected = part_own[step, piece] + part_in[step, piece]
            out_buf[step, :, cut] = (projected * gate_buf[step, 0:1, cut]).astype(jnp.bfloat16)
        copy = pltpu.make_async_copy(out_buf.at[step], out_hbm.at[step], out_sem.at[step])
        copy.start()
        return copy

    for step in range(steps):
        attend(step)
    copies = []
    for step in range(steps):
        project(step)
        copies.append(finish(step))

    for step in range(steps):
        for mask in range(1, peers):
            for kind in range(3):
                if step == 0 or mask < peers // 2:
                    send(step, kind, mask).wait_send()
            give_back(step, mask).wait_send()
        for piece in range(chunks):
            share(step, piece).wait_send()
    for copy in copies:
        copy.wait()


def fused_body(n_seq, n_head, query_field, key_field, value_field, positions, timesteps, w_out, w_time):
    steps, tokens, features = query_field.shape
    half = w_time.shape[1]
    peers = n_seq * n_head
    chunk = 512 if half % 512 == 0 else HD
    chunks = half // chunk
    bf16, f32 = jnp.bfloat16, jnp.float32
    dma = pltpu.SemaphoreType.DMA
    rope = jnp.asarray(feature_table())
    freq = jnp.asarray(time_table(w_time.shape[0] // 2))
    sizes = (n_seq, n_head, steps, tokens, half, chunk)
    scratch = [
        pltpu.VMEM(query_field.shape, bf16),
        pltpu.VMEM(key_field.shape, bf16),
        pltpu.VMEM(value_field.shape, bf16),
        pltpu.VMEM((1, tokens), jnp.int32),
        pltpu.VMEM((1, steps), jnp.int32),
        pltpu.VMEM(w_out.shape, bf16),
        pltpu.VMEM(w_time.shape, bf16),
        pltpu.VMEM(rope.shape, f32),
        pltpu.VMEM(freq.shape, f32),
        pltpu.VMEM((steps, 3, peers * tokens, HD), bf16),
        pltpu.VMEM((steps, 3, peers * tokens, HD), bf16),
        pltpu.VMEM((steps, peers * tokens, HD), bf16),
        pltpu.VMEM((steps, tokens, features), bf16),
        pltpu.VMEM((steps, chunks, tokens, chunk), f32),
        pltpu.VMEM((steps, chunks, tokens, chunk), f32),
        pltpu.VMEM((steps, chunks, tokens, chunk), f32),
        pltpu.VMEM((steps, tokens, half), bf16),
        pltpu.VMEM((steps, 8, half), f32),
        dma((9,)),
        dma((steps,)),
        dma((steps, 3, peers)),
        dma((steps, 3, peers)),
        dma((steps, peers)),
        dma((steps, peers)),
        dma((steps, chunks)),
        dma((steps, chunks)),
    ]
    return pl.pallas_call(
        lambda *refs: fused_kernel(sizes, *refs),
        out_shape=jax.ShapeDtypeStruct((steps, tokens, half), bf16),
        in_specs=[pl.BlockSpec(memory_space=pltpu.HBM)] * 9,
        out_specs=pl.BlockSpec(memory_space=pltpu.HBM),
        scratch_shapes=scratch,
        compiler_params=pltpu.CompilerParams(
            collective_id=0, has_side_effects=True, vmem_limit_bytes=56 * 1024 * 1024
        ),
    )(
        query_field,
        key_field,
        value_field,
        positions.reshape(1, tokens),
        timesteps.reshape(1, steps),
        w_out,
        w_time,
        rope,
        freq,
    )


def solution(mesh):
    placed = (
        P(None, ("group", "seq", "head"), "tp"),
        P(None, ("group", "seq", "head"), "tp"),
        P(None, ("group", "seq", "head"), "tp"),
        P(("group", "seq", "head")),
        P("group"),
        P("tp", None),
        P(None, "tp"),
    )
    n_seq, n_head = mesh.shape["seq"], mesh.shape["head"]
    peers = n_seq * n_head

    def chosen(query_field, *rest):
        local_heads = query_field.shape[2] // HD
        tokens = query_field.shape[1]
        if (
            local_heads == peers
            and peers & (peers - 1) == 0
            and peers >= 4
            and n_seq % 2 == 0
            and mesh.shape["tp"] == 2
            and tokens % 16 == 0
        ):
            return fused_body(n_seq, n_head, query_field, *rest)
        return body(query_field, *rest)

    return jax.shard_map(
        chosen,
        mesh=mesh,
        in_specs=placed,
        out_specs=P(None, ("group", "seq", "head"), "tp"),
        check_vma=False,
    )
```

```python
import math

import jax
import jax.numpy as jnp
import numpy as np
from jax import lax
from jax.experimental import pallas as pl
from jax.experimental.pallas import tpu as pltpu
from jax.sharding import PartitionSpec as P

HD = 128
LAT_H = 45
LAT_W = 80
STEPS = 2


rope_theta = 256.0
time_base = 10000.0
lowest = -1e30


def band_angles(positions):
    plane_size = LAT_H * LAT_W
    frame_index = positions // plane_size
    row_index = positions // LAT_W % LAT_H
    column_index = positions % LAT_W
    frame_band = HD // 8
    side_band = (HD - frame_band) // 2
    pieces = []
    for coordinate, band_width in (
        (frame_index, frame_band),
        (row_index, side_band),
        (column_index, side_band),
    ):
        pair_index = jnp.arange(band_width // 2, dtype=jnp.float32)
        frequency = rope_theta ** (-2.0 * pair_index / band_width)
        pieces.append(coordinate.astype(jnp.float32)[:, None] * frequency[None, :])
    return jnp.concatenate(pieces, axis=1)


def rotate(block_rows, cosine, sine_table):
    row_count = block_rows.shape[0]
    paired = block_rows.astype(jnp.float32).reshape(row_count, -1, HD // 2, 2)
    leading = paired[..., 0]
    second = paired[..., 1]
    cos_part = cosine[:, None, :]
    sin_part = sine_table[:, None, :]
    turned = jnp.stack(
        [leading * cos_part - second * sin_part, leading * sin_part + second * cos_part], axis=-1
    )
    return turned.reshape(row_count, -1).astype(jnp.bfloat16)


def encode(fresh, base_rows):
    row_count = fresh.shape[0]
    residual = (fresh.astype(jnp.float32) - base_rows.astype(jnp.float32)).reshape(
        row_count, -1, HD
    )
    largest = jnp.max(jnp.abs(residual), axis=2)
    code_scale = lax.optimization_barrier(((largest + 1e-06) / 120.0).astype(jnp.bfloat16))
    code_values = jnp.floor(residual / code_scale.astype(jnp.float32)[:, :, None] + 0.5)
    return (code_values.reshape(row_count, -1).astype(jnp.bfloat16), code_scale)


def decode_residual(code_values, code_scale, base_rows):
    row_count = code_values.shape[0]
    shaped = (
        code_values.astype(jnp.float32).reshape(row_count, -1, HD)
        * code_scale.astype(jnp.float32)[:, :, None]
    )
    return (base_rows.astype(jnp.float32) + shaped.reshape(row_count, -1)).astype(jnp.bfloat16)


def time_gate(step_value, w_time):
    half_feature_width = w_time.shape[0] // 2
    pair_index = jnp.arange(half_feature_width, dtype=jnp.float32)
    frequency = jnp.exp(-math.log(time_base) * pair_index / half_feature_width)
    phases = step_value.astype(jnp.float32) * frequency
    embedding = jnp.concatenate([jnp.cos(phases), jnp.sin(phases)])
    return jnp.sum(embedding[:, None] * w_time.astype(jnp.float32), axis=0)


def fold_update(fold_state, query_rows, key_piece, value_piece):
    running_max, running_sum, weighted = fold_state
    head_count = running_max.shape[0]
    score_scale = 1.0 / math.sqrt(HD)
    new_max, new_sum, new_weighted = ([], [], [])
    for head_index in range(head_count):
        lower = head_index * HD
        head_queries = query_rows[:, lower : lower + HD]
        head_keys = key_piece[:, lower : lower + HD]
        head_values = value_piece[:, lower : lower + HD]
        scores = (
            jnp.dot(head_queries, head_keys.T, preferred_element_type=jnp.float32) * score_scale
        )
        top_now = jnp.maximum(running_max[head_index], jnp.max(scores, axis=1))
        exponent = jnp.exp(scores - top_now[:, None])
        rescale = jnp.exp(running_max[head_index] - top_now)
        new_sum.append(running_sum[head_index] * rescale + jnp.sum(exponent, axis=1))
        mixed = jnp.dot(
            exponent.astype(jnp.bfloat16), head_values, preferred_element_type=jnp.float32
        )
        new_weighted.append(weighted[head_index] * rescale[:, None] + mixed)
        new_max.append(top_now)
    return (jnp.stack(new_max), jnp.stack(new_sum), jnp.stack(new_weighted))


def body(query_field, key_field, value_field, positions, timesteps, w_out, w_time):
    angles = band_angles(positions)
    cosine = jnp.cos(angles)
    sine_table = jnp.sin(angles)
    results = []
    own_keys = None
    own_values = None
    anchor_key_rows = None
    base_values = None
    for step_index in range(STEPS):
        rotated_q = rotate(query_field[step_index], cosine, sine_table)
        rotated_k = rotate(key_field[step_index], cosine, sine_table)
        fresh_values = value_field[step_index]
        query_rows, key_rows, value_rows = (
            lax.all_to_all(rotated_q, "head", split_axis=1, concat_axis=0, tiled=True),
            lax.all_to_all(rotated_k, "head", split_axis=1, concat_axis=0, tiled=True),
            lax.all_to_all(fresh_values, "head", split_axis=1, concat_axis=0, tiled=True),
        )
        head_count = query_rows.shape[1] // HD
        query_count = query_rows.shape[0]
        start_state = (
            jnp.full((head_count, query_count), lowest, jnp.float32),
            jnp.zeros((head_count, query_count), jnp.float32),
            jnp.zeros((head_count, query_count, HD), jnp.float32),
        )
        if step_index > 0:
            key_codes, key_scale = encode(key_rows, own_keys)
            value_codes, value_scale = encode(value_rows, own_values)
            own_keys = decode_residual(key_codes, key_scale, own_keys)
            own_values = decode_residual(value_codes, value_scale, own_values)
        if step_index == 0:
            anchor_key_rows, base_values = (
                lax.all_gather(key_rows, "seq", axis=0, tiled=True),
                lax.all_gather(value_rows, "seq", axis=0, tiled=True),
            )
            fold_state = fold_update(start_state, query_rows, anchor_key_rows, base_values)
        else:
            all_key_codes, all_value_codes, all_key_scales, all_value_scales = (
                lax.all_gather(key_codes, "seq", axis=0, tiled=True),
                lax.all_gather(value_codes, "seq", axis=0, tiled=True),
                lax.all_gather(key_scale, "seq", axis=0, tiled=True),
                lax.all_gather(value_scale, "seq", axis=0, tiled=True),
            )
            anchor_key_rows = decode_residual(all_key_codes, all_key_scales, anchor_key_rows)
            base_values = decode_residual(all_value_codes, all_value_scales, base_values)
            fold_state = fold_update(start_state, query_rows, anchor_key_rows, base_values)
        if step_index == 0:
            own_keys = key_rows
            own_values = value_rows
        running_max, running_sum, weighted = fold_state
        attended = (weighted / running_sum[:, :, None]).astype(jnp.bfloat16)
        attended = attended.transpose(1, 0, 2).reshape(query_count, head_count * HD)
        token_rows = lax.all_to_all(attended, "head", split_axis=0, concat_axis=1, tiled=True)
        partial_terms = jnp.dot(token_rows, w_out, preferred_element_type=jnp.float32)
        projected = lax.psum_scatter(partial_terms, "tp", scatter_dimension=1, tiled=True)
        gate_values = time_gate(timesteps[step_index], w_time)
        results.append((projected * gate_values[None, :]).astype(jnp.bfloat16))
    return jnp.stack(results)


MESH = pl.DeviceIdType.MESH


def feature_table():
    frame_band = HD // 8
    side_band = (HD - frame_band) // 2
    rope = []
    for band_width in (frame_band, side_band, side_band):
        pair_index = np.arange(band_width // 2)
        rope.append(np.repeat(rope_theta ** (-2.0 * pair_index / band_width), 2))
    table = np.zeros((8, HD), np.float32)
    table[0] = np.concatenate(rope)
    return table


def time_table(half_width):
    index = np.arange(half_width)
    table = np.zeros((8, half_width), np.float32)
    table[0] = np.exp(-math.log(time_base) * index / half_width)
    return table


def flipped(index, mask):
    out = index
    bit = 1
    while bit <= mask:
        if mask & bit:
            out = out + bit * (1 - 2 * ((index // bit) % 2))
        bit *= 2
    return out


def fused_kernel(
    sizes,
    q_hbm,
    k_hbm,
    v_hbm,
    pos_hbm,
    time_hbm,
    w_out_hbm,
    w_time_hbm,
    rope_hbm,
    freq_hbm,
    out_ref,
    q_in,
    k_in,
    v_in,
    pos_in,
    time_in,
    w_out,
    w_time,
    rope_in,
    freq_in,
    sent,
    got,
    att_out,
    att_in,
    part_out,
    part_in,
    part_own,
    gate_buf,
    load_sem,
    send_sem,
    recv_sem,
    att_send_sem,
    att_recv_sem,
    part_send_sem,
    part_recv_sem,
):
    n_seq, n_head, steps, tokens, half, chunk = sizes
    peers = n_seq * n_head
    chunks = half // chunk
    seq = lax.axis_index("seq")
    head = lax.axis_index("head")
    core = lax.axis_index("tp")
    me = seq * n_head + head

    loads = [
        pltpu.make_async_copy(source, target, load_sem.at[slot])
        for slot, (source, target) in enumerate(
            (
                (v_hbm, v_in),
                (pos_hbm, pos_in),
                (rope_hbm, rope_in),
                (k_hbm, k_in),
                (q_hbm, q_in),
                (time_hbm, time_in),
                (freq_hbm, freq_in),
                (w_time_hbm, w_time),
                (w_out_hbm, w_out),
            )
        )
    ]
    for load in loads:
        load.start()

    def place(mask):
        other = flipped(me, mask)
        return {"seq": other // n_head, "head": other % n_head}

    partner = {"tp": 1 - core}
    barrier = pltpu.get_barrier_semaphore()
    for mask in range(1, peers):
        pl.semaphore_signal(barrier, inc=1, device_id=place(mask), device_id_type=MESH)
    pl.semaphore_signal(barrier, inc=1, device_id=partner, device_id_type=MESH)

    order = list(range(peers - 1, -1, -1))

    def columns(mask):
        return pl.ds(pl.multiple_of(flipped(me, mask) * HD, HD), HD)

    def rows(mask):
        return pl.ds(mask * tokens, tokens)

    def send(step, kind, mask):
        if kind == 2 and step == 0:
            source = v_in.at[0, :, columns(mask)]
        else:
            source = sent.at[step, kind, rows(mask)]
        return pltpu.make_async_remote_copy(
            src_ref=source,
            dst_ref=got.at[step, kind, rows(mask)],
            send_sem=send_sem.at[step, kind, mask],
            recv_sem=recv_sem.at[step, kind, mask],
            device_id=place(mask),
            device_id_type=MESH,
        )

    def emit(step, kind, mask, block):
        if mask == 0:
            got[step, kind, rows(0)] = block
        else:
            sent[step, kind, rows(mask)] = block
            send(step, kind, mask).start()

    loads[1].wait()
    loads[2].wait()
    place_row = pos_in[...].astype(jnp.float32)
    square = (tokens, tokens)
    diagonal = lax.broadcasted_iota(jnp.int32, square, 0) == lax.broadcasted_iota(
        jnp.int32, square, 1
    )
    place_column = jnp.sum(
        jnp.where(diagonal, jnp.broadcast_to(place_row, square), 0.0), axis=1, keepdims=True
    )
    plane = float(LAT_H * LAT_W)
    line = jnp.floor((place_column + 0.5) * (1.0 / LAT_W))
    frame_index = jnp.floor((place_column + 0.5) * (1.0 / plane))
    row_index = line - frame_index * LAT_H
    column_index = place_column - line * LAT_W
    lane = lax.broadcasted_iota(jnp.int32, (tokens, HD), 1)
    frame_band = HD // 8
    side_band = (HD - frame_band) // 2
    coordinate = jnp.where(
        lane < frame_band,
        frame_index,
        jnp.where(lane < frame_band + side_band, row_index, column_index),
    )
    angles = coordinate * rope_in[0:1, :]
    cosine = jnp.cos(angles)
    even = lane % 2 == 0
    sine = jnp.where(even, -jnp.sin(angles), jnp.sin(angles))

    def turned(block):
        wide = block.astype(jnp.float32)
        swapped = jnp.where(even, pltpu.roll(wide, HD - 1, 1), pltpu.roll(wide, 1, 1))
        return (wide * cosine + swapped * sine).astype(jnp.bfloat16)

    def recoded(fresh, base):
        wide_base = base.astype(jnp.float32)
        residual = fresh.astype(jnp.float32) - wide_base
        largest = jnp.max(jnp.abs(residual), axis=1, keepdims=True)
        scale = ((largest + 1e-06) / 120.0).astype(jnp.bfloat16).astype(jnp.float32)
        code = jnp.floor(residual / scale + 0.5)
        return (wide_base + code * scale).astype(jnp.bfloat16)

    loads[0].wait()
    pl.semaphore_wait(barrier, peers)
    far = order[: peers // 2]
    near = order[peers // 2 :]

    def emit_values(step, masks):
        for mask in masks:
            if step == 0 and mask == 0:
                got[0, 2, rows(0)] = v_in[0, :, columns(0)]
            elif step == 0:
                send(0, 2, mask).start()
            else:
                block = recoded(v_in[step, :, columns(mask)], v_in[step - 1, :, columns(mask)])
                if step + 1 < steps:
                    v_in[step, :, columns(mask)] = block
                emit(step, 2, mask, block)

    def emit_keys(step, masks):
        for mask in masks:
            block = turned(k_in[step, :, columns(mask)])
            if step > 0:
                kept = got if mask == 0 else sent
                block = recoded(block, kept[step - 1, 1, rows(mask)])
            emit(step, 1, mask, block)

    def emit_queries(step, masks):
        for mask in masks:
            emit(step, 0, mask, turned(q_in[step, :, columns(mask)]))

    emit_values(0, far)
    loads[3].wait()
    emit_keys(0, far)
    loads[4].wait()
    emit_queries(0, far)
    emit_values(0, near)
    emit_keys(0, near)
    emit_queries(0, near)
    for step in range(1, steps):
        emit_values(step, far)
        emit_keys(step, far)
        emit_values(step, near)
        emit_keys(step, near)
        emit_queries(step, near)
        emit_queries(step, far)

    for load in loads[5:8]:
        load.wait()
    half_width = freq_in.shape[1]
    for step in range(steps):
        phases = time_in[0:1, step : step + 1].astype(jnp.float32) * freq_in[0:1, :]
        total = jnp.zeros((8, half), jnp.float32)
        for lower, wave in ((0, jnp.cos(phases)), (half_width, jnp.sin(phases))):
            first = wave.astype(jnp.bfloat16)
            rest = wave - first.astype(jnp.float32)
            second = rest.astype(jnp.bfloat16)
            third = (rest - second.astype(jnp.float32)).astype(jnp.bfloat16)
            which = lax.broadcasted_iota(jnp.int32, (8, half_width), 0)
            stacked = jnp.where(
                which == 0,
                first.astype(jnp.float32),
                jnp.where(
                    which == 1,
                    second.astype(jnp.float32),
                    jnp.where(which == 2, third.astype(jnp.float32), 0.0),
                ),
            ).astype(jnp.bfloat16)
            total = total + jnp.dot(
                stacked, w_time[lower : lower + half_width, :], preferred_element_type=jnp.float32
            )
        gate_buf[step] = jnp.broadcast_to(jnp.sum(total, axis=0, keepdims=True), (8, half))

    def give_back(step, mask):
        return pltpu.make_async_remote_copy(
            src_ref=att_out.at[step, rows(mask)],
            dst_ref=att_in.at[step, :, columns(0)],
            send_sem=att_send_sem.at[step, mask],
            recv_sem=att_recv_sem.at[step, mask],
            device_id=place(mask),
            device_id_type=MESH,
        )

    score_scale = 1.0 / math.sqrt(HD)

    def attend(step):
        last = step == steps - 1
        for kind in (2, 1):
            for mask in range(1, peers):
                send(step, kind, mask).wait_recv()
        keys = got[step, 1]
        values = got[step, 2]
        for start in range(0, peers, 2):
            for mask in (start, start + 1):
                if mask > 0:
                    send(step, 0, mask).wait_recv()
            queries = got[step, 0, start * tokens : (start + 2) * tokens]
            scores = (
                lax.dot_general(
                    queries, keys, (((1,), (1,)), ((), ())), preferred_element_type=jnp.float32
                )
                * score_scale
            )
            weights = jnp.exp(scores - jnp.max(scores, axis=1, keepdims=True))
            totals = jnp.sum(weights, axis=1, keepdims=True)
            mixed = jnp.dot(
                weights.astype(jnp.bfloat16), values, preferred_element_type=jnp.float32
            )
            attended = (mixed / totals).astype(jnp.bfloat16)
            for mask in (start, start + 1):
                block = attended[(mask - start) * tokens : (mask - start + 1) * tokens]
                if mask == 0:
                    att_in[step, :, columns(0)] = block
                else:
                    att_out[step, rows(mask)] = block
                    if last or mask < peers // 2:
                        give_back(step, mask).start()
        if not last:
            for kind in (2, 1, 0):
                for mask in far:
                    send(step + 1, kind, mask).wait_send()
            for mask in far:
                give_back(step, mask).start()

    def share(step, piece):
        return pltpu.make_async_remote_copy(
            src_ref=part_out.at[step, piece],
            dst_ref=part_in.at[step, piece],
            send_sem=part_send_sem.at[step, piece],
            recv_sem=part_recv_sem.at[step, piece],
            device_id=partner,
            device_id_type=MESH,
        )

    def project(step):
        depth = att_in.shape[2] // 2
        side = seq // (n_seq // 2)
        if step == 0:
            loads[8].wait()
        for masks, block in ((range(1, peers // 2), side), (range(peers // 2, peers), 1 - side)):
            for mask in masks:
                pltpu.make_async_remote_copy(
                    src_ref=att_out.at[step, rows(mask)],
                    dst_ref=att_in.at[step, :, columns(mask)],
                    send_sem=att_send_sem.at[step, mask],
                    recv_sem=att_recv_sem.at[step, mask],
                    device_id=place(mask),
                    device_id_type=MESH,
                ).wait_recv()
            features = pl.ds(pl.multiple_of(block * depth, depth), depth)
            attended = att_in[step, :, features]
            first = masks[0] == 1
            for target, part in ((1 - core, part_out), (core, part_own)):
                for piece in range(chunks):
                    lower = pl.multiple_of(target * half + piece * chunk, HD)
                    term = jnp.dot(
                        attended,
                        w_out[features, pl.ds(lower, chunk)],
                        preferred_element_type=jnp.float32,
                    )
                    part[step, piece] = term if first else part[step, piece] + term
                    if part is part_out and not first:
                        share(step, piece).start()

    def finish(step):
        for piece in range(chunks):
            share(step, piece).wait_recv()
            cut = slice(piece * chunk, (piece + 1) * chunk)
            projected = part_own[step, piece] + part_in[step, piece]
            out_ref[step, :, cut] = (projected * gate_buf[step, 0:1, cut]).astype(jnp.bfloat16)

    for step in range(steps):
        attend(step)
    for step in range(steps):
        project(step)
        finish(step)

    for step in range(steps):
        for mask in range(1, peers):
            for kind in range(3):
                if step == 0 or mask < peers // 2:
                    send(step, kind, mask).wait_send()
            give_back(step, mask).wait_send()
        for piece in range(chunks):
            share(step, piece).wait_send()


def fused_body(n_seq, n_head, query_field, key_field, value_field, positions, timesteps, w_out, w_time):
    steps, tokens, features = query_field.shape
    half = w_time.shape[1]
    peers = n_seq * n_head
    chunk = 512 if half % 512 == 0 else HD
    chunks = half // chunk
    bf16, f32 = jnp.bfloat16, jnp.float32
    dma = pltpu.SemaphoreType.DMA
    rope = jnp.asarray(feature_table())
    freq = jnp.asarray(time_table(w_time.shape[0] // 2))
    sizes = (n_seq, n_head, steps, tokens, half, chunk)
    scratch = [
        pltpu.VMEM(query_field.shape, bf16),
        pltpu.VMEM(key_field.shape, bf16),
        pltpu.VMEM(value_field.shape, bf16),
        pltpu.VMEM((1, tokens), jnp.int32),
        pltpu.VMEM((1, steps), jnp.int32),
        pltpu.VMEM(w_out.shape, bf16),
        pltpu.VMEM(w_time.shape, bf16),
        pltpu.VMEM(rope.shape, f32),
        pltpu.VMEM(freq.shape, f32),
        pltpu.VMEM((steps, 3, peers * tokens, HD), bf16),
        pltpu.VMEM((steps, 3, peers * tokens, HD), bf16),
        pltpu.VMEM((steps, peers * tokens, HD), bf16),
        pltpu.VMEM((steps, tokens, features), bf16),
        pltpu.VMEM((steps, chunks, tokens, chunk), f32),
        pltpu.VMEM((steps, chunks, tokens, chunk), f32),
        pltpu.VMEM((steps, chunks, tokens, chunk), f32),
        pltpu.VMEM((steps, 8, half), f32),
        dma((9,)),
        dma((steps, 3, peers)),
        dma((steps, 3, peers)),
        dma((steps, peers)),
        dma((steps, peers)),
        dma((steps, chunks)),
        dma((steps, chunks)),
    ]
    return pl.pallas_call(
        lambda *refs: fused_kernel(sizes, *refs),
        out_shape=pltpu.VMEM((steps, tokens, half), bf16),
        in_specs=[pl.BlockSpec(memory_space=pltpu.HBM)] * 9,
        out_specs=pl.BlockSpec(memory_space=pltpu.VMEM),
        scratch_shapes=scratch,
        compiler_params=pltpu.CompilerParams(
            collective_id=0, has_side_effects=True, vmem_limit_bytes=56 * 1024 * 1024
        ),
    )(
        query_field,
        key_field,
        value_field,
        positions.reshape(1, tokens),
        timesteps.reshape(1, steps),
        w_out,
        w_time,
        rope,
        freq,
    )


def solution(mesh):
    placed = (
        P(None, ("group", "seq", "head"), "tp"),
        P(None, ("group", "seq", "head"), "tp"),
        P(None, ("group", "seq", "head"), "tp"),
        P(("group", "seq", "head")),
        P("group"),
        P("tp", None),
        P(None, "tp"),
    )
    n_seq, n_head = mesh.shape["seq"], mesh.shape["head"]
    peers = n_seq * n_head

    def chosen(query_field, *rest):
        local_heads = query_field.shape[2] // HD
        tokens = query_field.shape[1]
        if (
            local_heads == peers
            and peers & (peers - 1) == 0
            and peers >= 4
            and n_seq % 2 == 0
            and mesh.shape["tp"] == 2
            and tokens % 16 == 0
        ):
            return fused_body(n_seq, n_head, query_field, *rest)
        return body(query_field, *rest)

    return jax.shard_map(
        chosen,
        mesh=mesh,
        in_specs=placed,
        out_specs=P(None, ("group", "seq", "head"), "tp"),
        check_vma=False,
    )
```

```python
import math

import jax
import jax.numpy as jnp
import numpy as np
from jax import lax
from jax.experimental import pallas as pl
from jax.experimental.pallas import tpu as pltpu
from jax.sharding import PartitionSpec as P

HD = 128
LAT_H = 45
LAT_W = 80
STEPS = 2


rope_theta = 256.0
time_base = 10000.0
lowest = -1e30


def band_angles(positions):
    plane_size = LAT_H * LAT_W
    frame_index = positions // plane_size
    row_index = positions // LAT_W % LAT_H
    column_index = positions % LAT_W
    frame_band = HD // 8
    side_band = (HD - frame_band) // 2
    pieces = []
    for coordinate, band_width in (
        (frame_index, frame_band),
        (row_index, side_band),
        (column_index, side_band),
    ):
        pair_index = jnp.arange(band_width // 2, dtype=jnp.float32)
        frequency = rope_theta ** (-2.0 * pair_index / band_width)
        pieces.append(coordinate.astype(jnp.float32)[:, None] * frequency[None, :])
    return jnp.concatenate(pieces, axis=1)


def rotate(block_rows, cosine, sine_table):
    row_count = block_rows.shape[0]
    paired = block_rows.astype(jnp.float32).reshape(row_count, -1, HD // 2, 2)
    leading = paired[..., 0]
    second = paired[..., 1]
    cos_part = cosine[:, None, :]
    sin_part = sine_table[:, None, :]
    turned = jnp.stack(
        [leading * cos_part - second * sin_part, leading * sin_part + second * cos_part], axis=-1
    )
    return turned.reshape(row_count, -1).astype(jnp.bfloat16)


def encode(fresh, base_rows):
    row_count = fresh.shape[0]
    residual = (fresh.astype(jnp.float32) - base_rows.astype(jnp.float32)).reshape(
        row_count, -1, HD
    )
    largest = jnp.max(jnp.abs(residual), axis=2)
    code_scale = lax.optimization_barrier(((largest + 1e-06) / 120.0).astype(jnp.bfloat16))
    code_values = jnp.floor(residual / code_scale.astype(jnp.float32)[:, :, None] + 0.5)
    return (code_values.reshape(row_count, -1).astype(jnp.bfloat16), code_scale)


def decode_residual(code_values, code_scale, base_rows):
    row_count = code_values.shape[0]
    shaped = (
        code_values.astype(jnp.float32).reshape(row_count, -1, HD)
        * code_scale.astype(jnp.float32)[:, :, None]
    )
    return (base_rows.astype(jnp.float32) + shaped.reshape(row_count, -1)).astype(jnp.bfloat16)


def time_gate(step_value, w_time):
    half_feature_width = w_time.shape[0] // 2
    pair_index = jnp.arange(half_feature_width, dtype=jnp.float32)
    frequency = jnp.exp(-math.log(time_base) * pair_index / half_feature_width)
    phases = step_value.astype(jnp.float32) * frequency
    embedding = jnp.concatenate([jnp.cos(phases), jnp.sin(phases)])
    return jnp.sum(embedding[:, None] * w_time.astype(jnp.float32), axis=0)


def fold_update(fold_state, query_rows, key_piece, value_piece):
    running_max, running_sum, weighted = fold_state
    head_count = running_max.shape[0]
    score_scale = 1.0 / math.sqrt(HD)
    new_max, new_sum, new_weighted = ([], [], [])
    for head_index in range(head_count):
        lower = head_index * HD
        head_queries = query_rows[:, lower : lower + HD]
        head_keys = key_piece[:, lower : lower + HD]
        head_values = value_piece[:, lower : lower + HD]
        scores = (
            jnp.dot(head_queries, head_keys.T, preferred_element_type=jnp.float32) * score_scale
        )
        top_now = jnp.maximum(running_max[head_index], jnp.max(scores, axis=1))
        exponent = jnp.exp(scores - top_now[:, None])
        rescale = jnp.exp(running_max[head_index] - top_now)
        new_sum.append(running_sum[head_index] * rescale + jnp.sum(exponent, axis=1))
        mixed = jnp.dot(
            exponent.astype(jnp.bfloat16), head_values, preferred_element_type=jnp.float32
        )
        new_weighted.append(weighted[head_index] * rescale[:, None] + mixed)
        new_max.append(top_now)
    return (jnp.stack(new_max), jnp.stack(new_sum), jnp.stack(new_weighted))


def body(query_field, key_field, value_field, positions, timesteps, w_out, w_time):
    angles = band_angles(positions)
    cosine = jnp.cos(angles)
    sine_table = jnp.sin(angles)
    results = []
    own_keys = None
    own_values = None
    anchor_key_rows = None
    base_values = None
    for step_index in range(STEPS):
        rotated_q = rotate(query_field[step_index], cosine, sine_table)
        rotated_k = rotate(key_field[step_index], cosine, sine_table)
        fresh_values = value_field[step_index]
        query_rows, key_rows, value_rows = (
            lax.all_to_all(rotated_q, "head", split_axis=1, concat_axis=0, tiled=True),
            lax.all_to_all(rotated_k, "head", split_axis=1, concat_axis=0, tiled=True),
            lax.all_to_all(fresh_values, "head", split_axis=1, concat_axis=0, tiled=True),
        )
        head_count = query_rows.shape[1] // HD
        query_count = query_rows.shape[0]
        start_state = (
            jnp.full((head_count, query_count), lowest, jnp.float32),
            jnp.zeros((head_count, query_count), jnp.float32),
            jnp.zeros((head_count, query_count, HD), jnp.float32),
        )
        if step_index > 0:
            key_codes, key_scale = encode(key_rows, own_keys)
            value_codes, value_scale = encode(value_rows, own_values)
            own_keys = decode_residual(key_codes, key_scale, own_keys)
            own_values = decode_residual(value_codes, value_scale, own_values)
        if step_index == 0:
            anchor_key_rows, base_values = (
                lax.all_gather(key_rows, "seq", axis=0, tiled=True),
                lax.all_gather(value_rows, "seq", axis=0, tiled=True),
            )
            fold_state = fold_update(start_state, query_rows, anchor_key_rows, base_values)
        else:
            all_key_codes, all_value_codes, all_key_scales, all_value_scales = (
                lax.all_gather(key_codes, "seq", axis=0, tiled=True),
                lax.all_gather(value_codes, "seq", axis=0, tiled=True),
                lax.all_gather(key_scale, "seq", axis=0, tiled=True),
                lax.all_gather(value_scale, "seq", axis=0, tiled=True),
            )
            anchor_key_rows = decode_residual(all_key_codes, all_key_scales, anchor_key_rows)
            base_values = decode_residual(all_value_codes, all_value_scales, base_values)
            fold_state = fold_update(start_state, query_rows, anchor_key_rows, base_values)
        if step_index == 0:
            own_keys = key_rows
            own_values = value_rows
        running_max, running_sum, weighted = fold_state
        attended = (weighted / running_sum[:, :, None]).astype(jnp.bfloat16)
        attended = attended.transpose(1, 0, 2).reshape(query_count, head_count * HD)
        token_rows = lax.all_to_all(attended, "head", split_axis=0, concat_axis=1, tiled=True)
        partial_terms = jnp.dot(token_rows, w_out, preferred_element_type=jnp.float32)
        projected = lax.psum_scatter(partial_terms, "tp", scatter_dimension=1, tiled=True)
        gate_values = time_gate(timesteps[step_index], w_time)
        results.append((projected * gate_values[None, :]).astype(jnp.bfloat16))
    return jnp.stack(results)


MESH = pl.DeviceIdType.MESH


def feature_table():
    frame_band = HD // 8
    side_band = (HD - frame_band) // 2
    rope = []
    for band_width in (frame_band, side_band, side_band):
        pair_index = np.arange(band_width // 2)
        rope.append(np.repeat(rope_theta ** (-2.0 * pair_index / band_width), 2))
    table = np.zeros((8, HD), np.float32)
    table[0] = np.concatenate(rope)
    return table


def time_table(half_width):
    index = np.arange(half_width)
    table = np.zeros((8, half_width), np.float32)
    table[0] = np.exp(-math.log(time_base) * index / half_width)
    return table


def flipped(index, mask):
    out = index
    bit = 1
    while bit <= mask:
        if mask & bit:
            out = out + bit * (1 - 2 * ((index // bit) % 2))
        bit *= 2
    return out


def fused_kernel(
    sizes,
    q_hbm,
    k_hbm,
    v_hbm,
    pos_hbm,
    time_hbm,
    w_out_hbm,
    w_time_hbm,
    rope_hbm,
    freq_hbm,
    out_ref,
    q_in,
    k_in,
    v_in,
    pos_in,
    time_in,
    w_out,
    w_time,
    rope_in,
    freq_in,
    sent,
    got,
    att_out,
    att_in,
    part_out,
    part_in,
    part_own,
    gate_buf,
    load_sem,
    send_sem,
    recv_sem,
    att_send_sem,
    att_recv_sem,
    part_send_sem,
    part_recv_sem,
    ready_sem,
):
    n_seq, n_head, steps, tokens, half, chunk = sizes
    peers = n_seq * n_head
    chunks = half // chunk
    seq = lax.axis_index("seq")
    head = lax.axis_index("head")
    core = lax.axis_index("tp")
    me = seq * n_head + head

    loads = [
        pltpu.make_async_copy(source, target, load_sem.at[slot])
        for slot, (source, target) in enumerate(
            (
                (v_hbm, v_in),
                (pos_hbm, pos_in),
                (rope_hbm, rope_in),
                (k_hbm, k_in),
                (q_hbm, q_in),
                (time_hbm, time_in),
                (freq_hbm, freq_in),
                (w_time_hbm, w_time),
                (w_out_hbm, w_out),
            )
        )
    ]
    for load in loads:
        load.start()

    def place(mask):
        other = flipped(me, mask)
        return {"seq": other // n_head, "head": other % n_head}

    partner = {"tp": 1 - core}
    barrier = pltpu.get_barrier_semaphore()
    beside, along, mirror = 1, n_head, (n_seq - 1) * n_head
    staged = n_seq == 4 and n_head == 2
    greeted = (beside, along, mirror) if staged else range(1, peers)
    for mask in greeted:
        pl.semaphore_signal(barrier, inc=1, device_id=place(mask), device_id_type=MESH)
    pl.semaphore_signal(barrier, inc=1, device_id=partner, device_id_type=MESH)

    def tell(slot, mask):
        pl.semaphore_signal(
            ready_sem.at[slot], inc=1, device_id=place(mask), device_id_type=MESH
        )


    order = list(range(peers - 1, -1, -1))

    def columns(mask):
        return pl.ds(pl.multiple_of(flipped(me, mask) * HD, HD), HD)

    def rows(mask):
        return pl.ds(mask * tokens, tokens)

    def send(step, kind, mask):
        if kind == 2 and step == 0:
            source = v_in.at[0, :, columns(mask)]
        else:
            source = sent.at[step, kind, rows(mask)]
        return pltpu.make_async_remote_copy(
            src_ref=source,
            dst_ref=got.at[step, kind, rows(mask)],
            send_sem=send_sem.at[step, kind, mask],
            recv_sem=recv_sem.at[step, kind, mask],
            device_id=place(mask),
            device_id_type=MESH,
        )

    def emit(step, kind, mask, block):
        if mask == 0:
            got[step, kind, rows(0)] = block
        else:
            sent[step, kind, rows(mask)] = block
            send(step, kind, mask).start()

    loads[1].wait()
    loads[2].wait()
    place_row = pos_in[...].astype(jnp.float32)
    square = (tokens, tokens)
    diagonal = lax.broadcasted_iota(jnp.int32, square, 0) == lax.broadcasted_iota(
        jnp.int32, square, 1
    )
    place_column = jnp.sum(
        jnp.where(diagonal, jnp.broadcast_to(place_row, square), 0.0), axis=1, keepdims=True
    )
    plane = float(LAT_H * LAT_W)
    line = jnp.floor((place_column + 0.5) * (1.0 / LAT_W))
    frame_index = jnp.floor((place_column + 0.5) * (1.0 / plane))
    row_index = line - frame_index * LAT_H
    column_index = place_column - line * LAT_W
    lane = lax.broadcasted_iota(jnp.int32, (tokens, HD), 1)
    frame_band = HD // 8
    side_band = (HD - frame_band) // 2
    coordinate = jnp.where(
        lane < frame_band,
        frame_index,
        jnp.where(lane < frame_band + side_band, row_index, column_index),
    )
    angles = coordinate * rope_in[0:1, :]
    cosine = jnp.cos(angles)
    even = lane % 2 == 0
    sine = jnp.where(even, -jnp.sin(angles), jnp.sin(angles))

    def turned(block):
        wide = block.astype(jnp.float32)
        swapped = jnp.where(even, pltpu.roll(wide, HD - 1, 1), pltpu.roll(wide, 1, 1))
        return (wide * cosine + swapped * sine).astype(jnp.bfloat16)

    def recoded(fresh, base):
        wide_base = base.astype(jnp.float32)
        residual = fresh.astype(jnp.float32) - wide_base
        largest = jnp.max(jnp.abs(residual), axis=1, keepdims=True)
        scale = ((largest + 1e-06) / 120.0).astype(jnp.bfloat16).astype(jnp.float32)
        code = jnp.floor(residual / scale + 0.5)
        return (wide_base + code * scale).astype(jnp.bfloat16)

    loads[0].wait()
    pl.semaphore_wait(barrier, len(greeted) + 1)
    if staged:
        tell(0, beside)
        tell(1, along)
    far = order[: peers // 2]
    near = order[peers // 2 :]

    def emit_values(step, masks):
        for mask in masks:
            if step == 0 and mask == 0:
                got[0, 2, rows(0)] = v_in[0, :, columns(0)]
            elif step == 0:
                send(0, 2, mask).start()
            else:
                block = recoded(v_in[step, :, columns(mask)], v_in[step - 1, :, columns(mask)])
                if step + 1 < steps:
                    v_in[step, :, columns(mask)] = block
                emit(step, 2, mask, block)

    def emit_keys(step, masks):
        for mask in masks:
            block = turned(k_in[step, :, columns(mask)])
            if step > 0:
                kept = got if mask == 0 else sent
                block = recoded(block, kept[step - 1, 1, rows(mask)])
            emit(step, 1, mask, block)

    def emit_queries(step, masks):
        for mask in masks:
            emit(step, 0, mask, turned(q_in[step, :, columns(mask)]))

    if staged:
        far = [mirror, mirror + beside, mirror - along, mirror - along + beside]
    for turn, mask in enumerate(far):
        if staged and turn == 1:
            pl.semaphore_wait(ready_sem.at[0], 1)
        if staged and turn == 2:
            pl.semaphore_wait(ready_sem.at[1], 1)
            tell(2, beside)
        if staged and turn == 3:
            pl.semaphore_wait(ready_sem.at[2], 1)
        emit_values(0, [mask])
        if turn == 0:
            loads[3].wait()
        emit_keys(0, [mask])
        if turn == 0:
            loads[4].wait()
        emit_queries(0, [mask])
    emit_values(0, near)
    emit_keys(0, near)
    emit_queries(0, near)
    for step in range(1, steps):
        emit_values(step, far)
        emit_keys(step, far)
        emit_values(step, near)
        emit_keys(step, near)
        emit_queries(step, near)
        emit_queries(step, far)

    for load in loads[5:8]:
        load.wait()
    half_width = freq_in.shape[1]
    for step in range(steps):
        phases = time_in[0:1, step : step + 1].astype(jnp.float32) * freq_in[0:1, :]
        total = jnp.zeros((8, half), jnp.float32)
        for lower, wave in ((0, jnp.cos(phases)), (half_width, jnp.sin(phases))):
            first = wave.astype(jnp.bfloat16)
            rest = wave - first.astype(jnp.float32)
            second = rest.astype(jnp.bfloat16)
            third = (rest - second.astype(jnp.float32)).astype(jnp.bfloat16)
            which = lax.broadcasted_iota(jnp.int32, (8, half_width), 0)
            stacked = jnp.where(
                which == 0,
                first.astype(jnp.float32),
                jnp.where(
                    which == 1,
                    second.astype(jnp.float32),
                    jnp.where(which == 2, third.astype(jnp.float32), 0.0),
                ),
            ).astype(jnp.bfloat16)
            total = total + jnp.dot(
                stacked, w_time[lower : lower + half_width, :], preferred_element_type=jnp.float32
            )
        gate_buf[step] = jnp.broadcast_to(jnp.sum(total, axis=0, keepdims=True), (8, half))

    def give_back(step, mask):
        return pltpu.make_async_remote_copy(
            src_ref=att_out.at[step, rows(mask)],
            dst_ref=att_in.at[step, :, columns(0)],
            send_sem=att_send_sem.at[step, mask],
            recv_sem=att_recv_sem.at[step, mask],
            device_id=place(mask),
            device_id_type=MESH,
        )

    score_scale = 1.0 / math.sqrt(HD)

    def attend(step):
        last = step == steps - 1
        for kind in (2, 1):
            for mask in range(1, peers):
                send(step, kind, mask).wait_recv()
        keys = got[step, 1]
        values = got[step, 2]
        for start in range(0, peers, 2):
            for mask in (start, start + 1):
                if mask > 0:
                    send(step, 0, mask).wait_recv()
            queries = got[step, 0, start * tokens : (start + 2) * tokens]
            scores = (
                lax.dot_general(
                    queries, keys, (((1,), (1,)), ((), ())), preferred_element_type=jnp.float32
                )
                * score_scale
            )
            weights = jnp.exp(scores - jnp.max(scores, axis=1, keepdims=True))
            totals = jnp.sum(weights, axis=1, keepdims=True)
            mixed = jnp.dot(
                weights.astype(jnp.bfloat16), values, preferred_element_type=jnp.float32
            )
            attended = (mixed / totals).astype(jnp.bfloat16)
            for mask in (start, start + 1):
                block = attended[(mask - start) * tokens : (mask - start + 1) * tokens]
                if mask == 0:
                    att_in[step, :, columns(0)] = block
                else:
                    att_out[step, rows(mask)] = block
                    if last or mask < peers // 2:
                        give_back(step, mask).start()
        if not last:
            for kind in (2, 1, 0):
                for mask in far:
                    send(step + 1, kind, mask).wait_send()
            for mask in far:
                give_back(step, mask).start()

    def share(step, piece):
        return pltpu.make_async_remote_copy(
            src_ref=part_out.at[step, piece],
            dst_ref=part_in.at[step, piece],
            send_sem=part_send_sem.at[step, piece],
            recv_sem=part_recv_sem.at[step, piece],
            device_id=partner,
            device_id_type=MESH,
        )

    def project(step):
        depth = att_in.shape[2] // 2
        side = seq // (n_seq // 2)
        if step == 0:
            loads[8].wait()
        for masks, block in ((range(1, peers // 2), side), (range(peers // 2, peers), 1 - side)):
            for mask in masks:
                pltpu.make_async_remote_copy(
                    src_ref=att_out.at[step, rows(mask)],
                    dst_ref=att_in.at[step, :, columns(mask)],
                    send_sem=att_send_sem.at[step, mask],
                    recv_sem=att_recv_sem.at[step, mask],
                    device_id=place(mask),
                    device_id_type=MESH,
                ).wait_recv()
            features = pl.ds(pl.multiple_of(block * depth, depth), depth)
            attended = att_in[step, :, features]
            first = masks[0] == 1
            for target, part in ((1 - core, part_out), (core, part_own)):
                for piece in range(chunks):
                    lower = pl.multiple_of(target * half + piece * chunk, HD)
                    term = jnp.dot(
                        attended,
                        w_out[features, pl.ds(lower, chunk)],
                        preferred_element_type=jnp.float32,
                    )
                    part[step, piece] = term if first else part[step, piece] + term
                    if part is part_out and not first:
                        share(step, piece).start()

    def finish(step):
        for piece in range(chunks):
            share(step, piece).wait_recv()
            cut = slice(piece * chunk, (piece + 1) * chunk)
            projected = part_own[step, piece] + part_in[step, piece]
            out_ref[step, :, cut] = (projected * gate_buf[step, 0:1, cut]).astype(jnp.bfloat16)

    for step in range(steps):
        attend(step)
    for step in range(steps):
        project(step)
        finish(step)

    for step in range(steps):
        for mask in range(1, peers):
            for kind in range(3):
                if step == 0 or mask < peers // 2:
                    send(step, kind, mask).wait_send()
            give_back(step, mask).wait_send()
        for piece in range(chunks):
            share(step, piece).wait_send()


def fused_body(n_seq, n_head, query_field, key_field, value_field, positions, timesteps, w_out, w_time):
    steps, tokens, features = query_field.shape
    half = w_time.shape[1]
    peers = n_seq * n_head
    chunk = 512 if half % 512 == 0 else HD
    chunks = half // chunk
    bf16, f32 = jnp.bfloat16, jnp.float32
    dma = pltpu.SemaphoreType.DMA
    rope = jnp.asarray(feature_table())
    freq = jnp.asarray(time_table(w_time.shape[0] // 2))
    sizes = (n_seq, n_head, steps, tokens, half, chunk)
    scratch = [
        pltpu.VMEM(query_field.shape, bf16),
        pltpu.VMEM(key_field.shape, bf16),
        pltpu.VMEM(value_field.shape, bf16),
        pltpu.VMEM((1, tokens), jnp.int32),
        pltpu.VMEM((1, steps), jnp.int32),
        pltpu.VMEM(w_out.shape, bf16),
        pltpu.VMEM(w_time.shape, bf16),
        pltpu.VMEM(rope.shape, f32),
        pltpu.VMEM(freq.shape, f32),
        pltpu.VMEM((steps, 3, peers * tokens, HD), bf16),
        pltpu.VMEM((steps, 3, peers * tokens, HD), bf16),
        pltpu.VMEM((steps, peers * tokens, HD), bf16),
        pltpu.VMEM((steps, tokens, features), bf16),
        pltpu.VMEM((steps, chunks, tokens, chunk), f32),
        pltpu.VMEM((steps, chunks, tokens, chunk), f32),
        pltpu.VMEM((steps, chunks, tokens, chunk), f32),
        pltpu.VMEM((steps, 8, half), f32),
        dma((9,)),
        dma((steps, 3, peers)),
        dma((steps, 3, peers)),
        dma((steps, peers)),
        dma((steps, peers)),
        dma((steps, chunks)),
        dma((steps, chunks)),
        pltpu.SemaphoreType.REGULAR((3,)),
    ]
    return pl.pallas_call(
        lambda *refs: fused_kernel(sizes, *refs),
        out_shape=pltpu.VMEM((steps, tokens, half), bf16),
        in_specs=[pl.BlockSpec(memory_space=pltpu.HBM)] * 9,
        out_specs=pl.BlockSpec(memory_space=pltpu.VMEM),
        scratch_shapes=scratch,
        compiler_params=pltpu.CompilerParams(
            collective_id=0, has_side_effects=True, vmem_limit_bytes=56 * 1024 * 1024
        ),
    )(
        query_field,
        key_field,
        value_field,
        positions.reshape(1, tokens),
        timesteps.reshape(1, steps),
        w_out,
        w_time,
        rope,
        freq,
    )


def solution(mesh):
    placed = (
        P(None, ("group", "seq", "head"), "tp"),
        P(None, ("group", "seq", "head"), "tp"),
        P(None, ("group", "seq", "head"), "tp"),
        P(("group", "seq", "head")),
        P("group"),
        P("tp", None),
        P(None, "tp"),
    )
    n_seq, n_head = mesh.shape["seq"], mesh.shape["head"]
    peers = n_seq * n_head

    def chosen(query_field, *rest):
        local_heads = query_field.shape[2] // HD
        tokens = query_field.shape[1]
        if (
            local_heads == peers
            and peers & (peers - 1) == 0
            and peers >= 4
            and n_seq % 2 == 0
            and mesh.shape["tp"] == 2
            and tokens % 16 == 0
        ):
            return fused_body(n_seq, n_head, query_field, *rest)
        return body(query_field, *rest)

    return jax.shard_map(
        chosen,
        mesh=mesh,
        in_specs=placed,
        out_specs=P(None, ("group", "seq", "head"), "tp"),
        check_vma=False,
    )
```

```python
import math

import jax
import jax.numpy as jnp
import numpy as np
from jax import lax
from jax.experimental import pallas as pl
from jax.experimental.pallas import tpu as pltpu
from jax.sharding import PartitionSpec as P

HD = 128
LAT_H = 45
LAT_W = 80
STEPS = 2


rope_theta = 256.0
time_base = 10000.0
lowest = -1e30


def band_angles(positions):
    plane_size = LAT_H * LAT_W
    frame_index = positions // plane_size
    row_index = positions // LAT_W % LAT_H
    column_index = positions % LAT_W
    frame_band = HD // 8
    side_band = (HD - frame_band) // 2
    pieces = []
    for coordinate, band_width in (
        (frame_index, frame_band),
        (row_index, side_band),
        (column_index, side_band),
    ):
        pair_index = jnp.arange(band_width // 2, dtype=jnp.float32)
        frequency = rope_theta ** (-2.0 * pair_index / band_width)
        pieces.append(coordinate.astype(jnp.float32)[:, None] * frequency[None, :])
    return jnp.concatenate(pieces, axis=1)


def rotate(block_rows, cosine, sine_table):
    row_count = block_rows.shape[0]
    paired = block_rows.astype(jnp.float32).reshape(row_count, -1, HD // 2, 2)
    leading = paired[..., 0]
    second = paired[..., 1]
    cos_part = cosine[:, None, :]
    sin_part = sine_table[:, None, :]
    turned = jnp.stack(
        [leading * cos_part - second * sin_part, leading * sin_part + second * cos_part], axis=-1
    )
    return turned.reshape(row_count, -1).astype(jnp.bfloat16)


def encode(fresh, base_rows):
    row_count = fresh.shape[0]
    residual = (fresh.astype(jnp.float32) - base_rows.astype(jnp.float32)).reshape(
        row_count, -1, HD
    )
    largest = jnp.max(jnp.abs(residual), axis=2)
    code_scale = lax.optimization_barrier(((largest + 1e-06) / 120.0).astype(jnp.bfloat16))
    code_values = jnp.floor(residual / code_scale.astype(jnp.float32)[:, :, None] + 0.5)
    return (code_values.reshape(row_count, -1).astype(jnp.bfloat16), code_scale)


def decode_residual(code_values, code_scale, base_rows):
    row_count = code_values.shape[0]
    shaped = (
        code_values.astype(jnp.float32).reshape(row_count, -1, HD)
        * code_scale.astype(jnp.float32)[:, :, None]
    )
    return (base_rows.astype(jnp.float32) + shaped.reshape(row_count, -1)).astype(jnp.bfloat16)


def time_gate(step_value, w_time):
    half_feature_width = w_time.shape[0] // 2
    pair_index = jnp.arange(half_feature_width, dtype=jnp.float32)
    frequency = jnp.exp(-math.log(time_base) * pair_index / half_feature_width)
    phases = step_value.astype(jnp.float32) * frequency
    embedding = jnp.concatenate([jnp.cos(phases), jnp.sin(phases)])
    return jnp.sum(embedding[:, None] * w_time.astype(jnp.float32), axis=0)


def fold_update(fold_state, query_rows, key_piece, value_piece):
    running_max, running_sum, weighted = fold_state
    head_count = running_max.shape[0]
    score_scale = 1.0 / math.sqrt(HD)
    new_max, new_sum, new_weighted = ([], [], [])
    for head_index in range(head_count):
        lower = head_index * HD
        head_queries = query_rows[:, lower : lower + HD]
        head_keys = key_piece[:, lower : lower + HD]
        head_values = value_piece[:, lower : lower + HD]
        scores = (
            jnp.dot(head_queries, head_keys.T, preferred_element_type=jnp.float32) * score_scale
        )
        top_now = jnp.maximum(running_max[head_index], jnp.max(scores, axis=1))
        exponent = jnp.exp(scores - top_now[:, None])
        rescale = jnp.exp(running_max[head_index] - top_now)
        new_sum.append(running_sum[head_index] * rescale + jnp.sum(exponent, axis=1))
        mixed = jnp.dot(
            exponent.astype(jnp.bfloat16), head_values, preferred_element_type=jnp.float32
        )
        new_weighted.append(weighted[head_index] * rescale[:, None] + mixed)
        new_max.append(top_now)
    return (jnp.stack(new_max), jnp.stack(new_sum), jnp.stack(new_weighted))


def body(query_field, key_field, value_field, positions, timesteps, w_out, w_time):
    angles = band_angles(positions)
    cosine = jnp.cos(angles)
    sine_table = jnp.sin(angles)
    results = []
    own_keys = None
    own_values = None
    anchor_key_rows = None
    base_values = None
    for step_index in range(STEPS):
        rotated_q = rotate(query_field[step_index], cosine, sine_table)
        rotated_k = rotate(key_field[step_index], cosine, sine_table)
        fresh_values = value_field[step_index]
        query_rows, key_rows, value_rows = (
            lax.all_to_all(rotated_q, "head", split_axis=1, concat_axis=0, tiled=True),
            lax.all_to_all(rotated_k, "head", split_axis=1, concat_axis=0, tiled=True),
            lax.all_to_all(fresh_values, "head", split_axis=1, concat_axis=0, tiled=True),
        )
        head_count = query_rows.shape[1] // HD
        query_count = query_rows.shape[0]
        start_state = (
            jnp.full((head_count, query_count), lowest, jnp.float32),
            jnp.zeros((head_count, query_count), jnp.float32),
            jnp.zeros((head_count, query_count, HD), jnp.float32),
        )
        if step_index > 0:
            key_codes, key_scale = encode(key_rows, own_keys)
            value_codes, value_scale = encode(value_rows, own_values)
            own_keys = decode_residual(key_codes, key_scale, own_keys)
            own_values = decode_residual(value_codes, value_scale, own_values)
        if step_index == 0:
            anchor_key_rows, base_values = (
                lax.all_gather(key_rows, "seq", axis=0, tiled=True),
                lax.all_gather(value_rows, "seq", axis=0, tiled=True),
            )
            fold_state = fold_update(start_state, query_rows, anchor_key_rows, base_values)
        else:
            all_key_codes, all_value_codes, all_key_scales, all_value_scales = (
                lax.all_gather(key_codes, "seq", axis=0, tiled=True),
                lax.all_gather(value_codes, "seq", axis=0, tiled=True),
                lax.all_gather(key_scale, "seq", axis=0, tiled=True),
                lax.all_gather(value_scale, "seq", axis=0, tiled=True),
            )
            anchor_key_rows = decode_residual(all_key_codes, all_key_scales, anchor_key_rows)
            base_values = decode_residual(all_value_codes, all_value_scales, base_values)
            fold_state = fold_update(start_state, query_rows, anchor_key_rows, base_values)
        if step_index == 0:
            own_keys = key_rows
            own_values = value_rows
        running_max, running_sum, weighted = fold_state
        attended = (weighted / running_sum[:, :, None]).astype(jnp.bfloat16)
        attended = attended.transpose(1, 0, 2).reshape(query_count, head_count * HD)
        token_rows = lax.all_to_all(attended, "head", split_axis=0, concat_axis=1, tiled=True)
        partial_terms = jnp.dot(token_rows, w_out, preferred_element_type=jnp.float32)
        projected = lax.psum_scatter(partial_terms, "tp", scatter_dimension=1, tiled=True)
        gate_values = time_gate(timesteps[step_index], w_time)
        results.append((projected * gate_values[None, :]).astype(jnp.bfloat16))
    return jnp.stack(results)


MESH = pl.DeviceIdType.MESH


def feature_table():
    frame_band = HD // 8
    side_band = (HD - frame_band) // 2
    rope = []
    for band_width in (frame_band, side_band, side_band):
        pair_index = np.arange(band_width // 2)
        rope.append(np.repeat(rope_theta ** (-2.0 * pair_index / band_width), 2))
    table = np.zeros((8, HD), np.float32)
    table[0] = np.concatenate(rope)
    return table


def time_table(half_width):
    index = np.arange(half_width)
    table = np.zeros((8, half_width), np.float32)
    table[0] = np.exp(-math.log(time_base) * index / half_width)
    return table


def flipped(index, mask):
    out = index
    bit = 1
    while bit <= mask:
        if mask & bit:
            out = out + bit * (1 - 2 * ((index // bit) % 2))
        bit *= 2
    return out


def fused_kernel(
    sizes,
    q_hbm,
    k_hbm,
    v_hbm,
    pos_hbm,
    time_hbm,
    w_out_hbm,
    w_time_hbm,
    rope_hbm,
    freq_hbm,
    out_ref,
    q_in,
    k_in,
    v_in,
    pos_in,
    time_in,
    w_out,
    w_time,
    rope_in,
    freq_in,
    sent,
    got,
    att_out,
    att_in,
    part_out,
    part_in,
    part_own,
    gate_buf,
    load_sem,
    send_sem,
    recv_sem,
    att_send_sem,
    att_recv_sem,
    part_send_sem,
    part_recv_sem,
    ready_sem,
):
    n_seq, n_head, steps, tokens, half, chunk = sizes
    peers = n_seq * n_head
    chunks = half // chunk
    seq = lax.axis_index("seq")
    head = lax.axis_index("head")
    core = lax.axis_index("tp")
    me = seq * n_head + head

    loads = [
        pltpu.make_async_copy(source, target, load_sem.at[slot])
        for slot, (source, target) in enumerate(
            (
                (v_hbm, v_in),
                (pos_hbm, pos_in),
                (rope_hbm, rope_in),
                (k_hbm, k_in),
                (q_hbm, q_in),
                (time_hbm, time_in),
                (freq_hbm, freq_in),
                (w_time_hbm, w_time),
                (w_out_hbm, w_out),
            )
        )
    ]
    for load in loads:
        load.start()

    def place(mask):
        other = flipped(me, mask)
        return {"seq": other // n_head, "head": other % n_head}

    partner = {"tp": 1 - core}
    barrier = pltpu.get_barrier_semaphore()
    beside, along, mirror = 1, n_head, (n_seq - 1) * n_head
    staged = n_seq == 4 and n_head == 2
    greeted = (beside, along, mirror) if staged else range(1, peers)
    for mask in greeted:
        pl.semaphore_signal(barrier, inc=1, device_id=place(mask), device_id_type=MESH)
    pl.semaphore_signal(barrier, inc=1, device_id=partner, device_id_type=MESH)

    def tell(slot, mask):
        pl.semaphore_signal(
            ready_sem.at[slot], inc=1, device_id=place(mask), device_id_type=MESH
        )


    order = list(range(peers - 1, -1, -1))

    def columns(mask):
        return pl.ds(pl.multiple_of(flipped(me, mask) * HD, HD), HD)

    def rows(mask):
        return pl.ds(mask * tokens, tokens)

    def send(step, kind, mask):
        if kind == 2 and step == 0:
            source = v_in.at[0, :, columns(mask)]
        else:
            source = sent.at[step, kind, rows(mask)]
        return pltpu.make_async_remote_copy(
            src_ref=source,
            dst_ref=got.at[step, kind, rows(mask)],
            send_sem=send_sem.at[step, kind, mask],
            recv_sem=recv_sem.at[step, kind, mask],
            device_id=place(mask),
            device_id_type=MESH,
        )

    def emit(step, kind, mask, block):
        if mask == 0:
            got[step, kind, rows(0)] = block
        else:
            sent[step, kind, rows(mask)] = block
            send(step, kind, mask).start()

    loads[1].wait()
    loads[2].wait()
    place_row = pos_in[...].astype(jnp.float32)
    square = (tokens, tokens)
    diagonal = lax.broadcasted_iota(jnp.int32, square, 0) == lax.broadcasted_iota(
        jnp.int32, square, 1
    )
    place_column = jnp.sum(
        jnp.where(diagonal, jnp.broadcast_to(place_row, square), 0.0), axis=1, keepdims=True
    )
    plane = float(LAT_H * LAT_W)
    line = jnp.floor((place_column + 0.5) * (1.0 / LAT_W))
    frame_index = jnp.floor((place_column + 0.5) * (1.0 / plane))
    row_index = line - frame_index * LAT_H
    column_index = place_column - line * LAT_W
    lane = lax.broadcasted_iota(jnp.int32, (tokens, HD), 1)
    frame_band = HD // 8
    side_band = (HD - frame_band) // 2
    coordinate = jnp.where(
        lane < frame_band,
        frame_index,
        jnp.where(lane < frame_band + side_band, row_index, column_index),
    )
    angles = coordinate * rope_in[0:1, :]
    cosine = jnp.cos(angles)
    even = lane % 2 == 0
    sine = jnp.where(even, -jnp.sin(angles), jnp.sin(angles))

    def turned(block):
        wide = block.astype(jnp.float32)
        swapped = jnp.where(even, pltpu.roll(wide, HD - 1, 1), pltpu.roll(wide, 1, 1))
        return (wide * cosine + swapped * sine).astype(jnp.bfloat16)

    def recoded(fresh, base):
        wide_base = base.astype(jnp.float32)
        residual = fresh.astype(jnp.float32) - wide_base
        largest = jnp.max(jnp.abs(residual), axis=1, keepdims=True)
        scale = ((largest + 1e-06) / 120.0).astype(jnp.bfloat16).astype(jnp.float32)
        code = jnp.floor(residual / scale + 0.5)
        return (wide_base + code * scale).astype(jnp.bfloat16)

    loads[0].wait()
    pl.semaphore_wait(barrier, len(greeted) + 1)
    if staged:
        tell(0, beside)
        tell(1, along)
    far = order[: peers // 2]
    near = order[peers // 2 :]

    def emit_values(step, masks):
        for mask in masks:
            if step == 0 and mask == 0:
                got[0, 2, rows(0)] = v_in[0, :, columns(0)]
            elif step == 0:
                send(0, 2, mask).start()
            else:
                block = recoded(v_in[step, :, columns(mask)], v_in[step - 1, :, columns(mask)])
                if step + 1 < steps:
                    v_in[step, :, columns(mask)] = block
                emit(step, 2, mask, block)

    def emit_keys(step, masks):
        for mask in masks:
            block = turned(k_in[step, :, columns(mask)])
            if step > 0:
                kept = got if mask == 0 else sent
                block = recoded(block, kept[step - 1, 1, rows(mask)])
            emit(step, 1, mask, block)

    def emit_queries(step, masks):
        for mask in masks:
            emit(step, 0, mask, turned(q_in[step, :, columns(mask)]))

    if staged:
        far = [mirror, mirror + beside, mirror - along, mirror - along + beside]
    for turn, mask in enumerate(far):
        if staged and turn == 1:
            pl.semaphore_wait(ready_sem.at[0], 1)
        if staged and turn == 2:
            pl.semaphore_wait(ready_sem.at[1], 1)
            tell(2, beside)
        if staged and turn == 3:
            pl.semaphore_wait(ready_sem.at[2], 1)
        emit_values(0, [mask])
        if turn == 0:
            loads[3].wait()
        emit_keys(0, [mask])
        if turn == 0:
            loads[4].wait()
        emit_queries(0, [mask])
        if turn == 0 and staged and steps > 1:
            emit_values(1, [mask])
            emit_keys(1, [mask])
    emit_values(0, near)
    emit_keys(0, near)
    emit_queries(0, near)
    for step in range(1, steps):
        late = far[1:] if staged and step == 1 else far
        emit_values(step, late)
        emit_keys(step, late)
        emit_values(step, near)
        emit_keys(step, near)
        emit_queries(step, near)
        emit_queries(step, far)

    for load in loads[5:8]:
        load.wait()
    half_width = freq_in.shape[1]
    for step in range(steps):
        phases = time_in[0:1, step : step + 1].astype(jnp.float32) * freq_in[0:1, :]
        total = jnp.zeros((8, half), jnp.float32)
        for lower, wave in ((0, jnp.cos(phases)), (half_width, jnp.sin(phases))):
            first = wave.astype(jnp.bfloat16)
            rest = wave - first.astype(jnp.float32)
            second = rest.astype(jnp.bfloat16)
            third = (rest - second.astype(jnp.float32)).astype(jnp.bfloat16)
            which = lax.broadcasted_iota(jnp.int32, (8, half_width), 0)
            stacked = jnp.where(
                which == 0,
                first.astype(jnp.float32),
                jnp.where(
                    which == 1,
                    second.astype(jnp.float32),
                    jnp.where(which == 2, third.astype(jnp.float32), 0.0),
                ),
            ).astype(jnp.bfloat16)
            total = total + jnp.dot(
                stacked, w_time[lower : lower + half_width, :], preferred_element_type=jnp.float32
            )
        gate_buf[step] = jnp.broadcast_to(jnp.sum(total, axis=0, keepdims=True), (8, half))

    def give_back(step, mask):
        return pltpu.make_async_remote_copy(
            src_ref=att_out.at[step, rows(mask)],
            dst_ref=att_in.at[step, :, columns(0)],
            send_sem=att_send_sem.at[step, mask],
            recv_sem=att_recv_sem.at[step, mask],
            device_id=place(mask),
            device_id_type=MESH,
        )

    score_scale = 1.0 / math.sqrt(HD)

    def attend(step):
        for kind in (2, 1):
            for mask in range(1, peers):
                send(step, kind, mask).wait_recv()
        keys = got[step, 1]
        values = got[step, 2]
        for start in range(0, peers, 2):
            for mask in (start, start + 1):
                if mask > 0:
                    send(step, 0, mask).wait_recv()
            queries = got[step, 0, start * tokens : (start + 2) * tokens]
            scores = (
                lax.dot_general(
                    queries, keys, (((1,), (1,)), ((), ())), preferred_element_type=jnp.float32
                )
                * score_scale
            )
            weights = jnp.exp(scores - jnp.max(scores, axis=1, keepdims=True))
            totals = jnp.sum(weights, axis=1, keepdims=True)
            mixed = jnp.dot(
                weights.astype(jnp.bfloat16), values, preferred_element_type=jnp.float32
            )
            attended = (mixed / totals).astype(jnp.bfloat16)
            for mask in (start, start + 1):
                block = attended[(mask - start) * tokens : (mask - start + 1) * tokens]
                if mask == 0:
                    att_in[step, :, columns(0)] = block
                else:
                    att_out[step, rows(mask)] = block
                    give_back(step, mask).start()

    def share(step, piece):
        return pltpu.make_async_remote_copy(
            src_ref=part_out.at[step, piece],
            dst_ref=part_in.at[step, piece],
            send_sem=part_send_sem.at[step, piece],
            recv_sem=part_recv_sem.at[step, piece],
            device_id=partner,
            device_id_type=MESH,
        )

    def project(step):
        depth = att_in.shape[2] // 2
        side = seq // (n_seq // 2)
        if step == 0:
            loads[8].wait()
        for masks, block in ((range(1, peers // 2), side), (range(peers // 2, peers), 1 - side)):
            for mask in masks:
                pltpu.make_async_remote_copy(
                    src_ref=att_out.at[step, rows(mask)],
                    dst_ref=att_in.at[step, :, columns(mask)],
                    send_sem=att_send_sem.at[step, mask],
                    recv_sem=att_recv_sem.at[step, mask],
                    device_id=place(mask),
                    device_id_type=MESH,
                ).wait_recv()
            features = pl.ds(pl.multiple_of(block * depth, depth), depth)
            attended = att_in[step, :, features]
            first = masks[0] == 1
            for target, part in ((1 - core, part_out), (core, part_own)):
                for piece in range(chunks):
                    lower = pl.multiple_of(target * half + piece * chunk, HD)
                    term = jnp.dot(
                        attended,
                        w_out[features, pl.ds(lower, chunk)],
                        preferred_element_type=jnp.float32,
                    )
                    part[step, piece] = (term if first else part[step, piece] + term).astype(part.dtype)
                    if part is part_out and not first:
                        share(step, piece).start()

    def finish(step):
        for piece in range(chunks):
            share(step, piece).wait_recv()
            cut = slice(piece * chunk, (piece + 1) * chunk)
            projected = part_own[step, piece] + part_in[step, piece]
            out_ref[step, :, cut] = (projected * gate_buf[step, 0:1, cut]).astype(jnp.bfloat16)

    for step in range(steps):
        attend(step)
    for step in range(steps):
        project(step)
        finish(step)

    for step in range(steps):
        for mask in range(1, peers):
            for kind in range(3):
                send(step, kind, mask).wait_send()
            give_back(step, mask).wait_send()
        for piece in range(chunks):
            share(step, piece).wait_send()


def fused_body(n_seq, n_head, query_field, key_field, value_field, positions, timesteps, w_out, w_time):
    steps, tokens, features = query_field.shape
    half = w_time.shape[1]
    peers = n_seq * n_head
    chunk = 512 if half % 512 == 0 else HD
    chunks = half // chunk
    bf16, f32 = jnp.bfloat16, jnp.float32
    dma = pltpu.SemaphoreType.DMA
    rope = jnp.asarray(feature_table())
    freq = jnp.asarray(time_table(w_time.shape[0] // 2))
    sizes = (n_seq, n_head, steps, tokens, half, chunk)
    scratch = [
        pltpu.VMEM(query_field.shape, bf16),
        pltpu.VMEM(key_field.shape, bf16),
        pltpu.VMEM(value_field.shape, bf16),
        pltpu.VMEM((1, tokens), jnp.int32),
        pltpu.VMEM((1, steps), jnp.int32),
        pltpu.VMEM(w_out.shape, bf16),
        pltpu.VMEM(w_time.shape, bf16),
        pltpu.VMEM(rope.shape, f32),
        pltpu.VMEM(freq.shape, f32),
        pltpu.VMEM((steps, 3, peers * tokens, HD), bf16),
        pltpu.VMEM((steps, 3, peers * tokens, HD), bf16),
        pltpu.VMEM((steps, peers * tokens, HD), bf16),
        pltpu.VMEM((steps, tokens, features), bf16),
        pltpu.VMEM((steps, chunks, tokens, chunk), bf16),
        pltpu.VMEM((steps, chunks, tokens, chunk), bf16),
        pltpu.VMEM((steps, chunks, tokens, chunk), f32),
        pltpu.VMEM((steps, 8, half), f32),
        dma((9,)),
        dma((steps, 3, peers)),
        dma((steps, 3, peers)),
        dma((steps, peers)),
        dma((steps, peers)),
        dma((steps, chunks)),
        dma((steps, chunks)),
        pltpu.SemaphoreType.REGULAR((3,)),
    ]
    return pl.pallas_call(
        lambda *refs: fused_kernel(sizes, *refs),
        out_shape=pltpu.VMEM((steps, tokens, half), bf16),
        in_specs=[pl.BlockSpec(memory_space=pltpu.HBM)] * 9,
        out_specs=pl.BlockSpec(memory_space=pltpu.VMEM),
        scratch_shapes=scratch,
        compiler_params=pltpu.CompilerParams(
            collective_id=0, has_side_effects=True, vmem_limit_bytes=56 * 1024 * 1024
        ),
    )(
        query_field,
        key_field,
        value_field,
        positions.reshape(1, tokens),
        timesteps.reshape(1, steps),
        w_out,
        w_time,
        rope,
        freq,
    )


def solution(mesh):
    placed = (
        P(None, ("group", "seq", "head"), "tp"),
        P(None, ("group", "seq", "head"), "tp"),
        P(None, ("group", "seq", "head"), "tp"),
        P(("group", "seq", "head")),
        P("group"),
        P("tp", None),
        P(None, "tp"),
    )
    n_seq, n_head = mesh.shape["seq"], mesh.shape["head"]
    peers = n_seq * n_head

    def chosen(query_field, *rest):
        local_heads = query_field.shape[2] // HD
        tokens = query_field.shape[1]
        if (
            local_heads == peers
            and peers & (peers - 1) == 0
            and peers >= 4
            and n_seq % 2 == 0
            and mesh.shape["tp"] == 2
            and tokens % 16 == 0
        ):
            return fused_body(n_seq, n_head, query_field, *rest)
        return body(query_field, *rest)

    return jax.shard_map(
        chosen,
        mesh=mesh,
        in_specs=placed,
        out_specs=P(None, ("group", "seq", "head"), "tp"),
        check_vma=False,
    )
```

```python
import math

import jax
import jax.numpy as jnp
import numpy as np
from jax import lax
from jax.experimental import pallas as pl
from jax.experimental.pallas import tpu as pltpu
from jax.sharding import PartitionSpec as P

HD = 128
LAT_H = 45
LAT_W = 80
STEPS = 2


rope_theta = 256.0
time_base = 10000.0
lowest = -1e30


def band_angles(positions):
    plane_size = LAT_H * LAT_W
    frame_index = positions // plane_size
    row_index = positions // LAT_W % LAT_H
    column_index = positions % LAT_W
    frame_band = HD // 8
    side_band = (HD - frame_band) // 2
    pieces = []
    for coordinate, band_width in (
        (frame_index, frame_band),
        (row_index, side_band),
        (column_index, side_band),
    ):
        pair_index = jnp.arange(band_width // 2, dtype=jnp.float32)
        frequency = rope_theta ** (-2.0 * pair_index / band_width)
        pieces.append(coordinate.astype(jnp.float32)[:, None] * frequency[None, :])
    return jnp.concatenate(pieces, axis=1)


def rotate(block_rows, cosine, sine_table):
    row_count = block_rows.shape[0]
    paired = block_rows.astype(jnp.float32).reshape(row_count, -1, HD // 2, 2)
    leading = paired[..., 0]
    second = paired[..., 1]
    cos_part = cosine[:, None, :]
    sin_part = sine_table[:, None, :]
    turned = jnp.stack(
        [leading * cos_part - second * sin_part, leading * sin_part + second * cos_part], axis=-1
    )
    return turned.reshape(row_count, -1).astype(jnp.bfloat16)


def encode(fresh, base_rows):
    row_count = fresh.shape[0]
    residual = (fresh.astype(jnp.float32) - base_rows.astype(jnp.float32)).reshape(
        row_count, -1, HD
    )
    largest = jnp.max(jnp.abs(residual), axis=2)
    code_scale = lax.optimization_barrier(((largest + 1e-06) / 120.0).astype(jnp.bfloat16))
    code_values = jnp.floor(residual / code_scale.astype(jnp.float32)[:, :, None] + 0.5)
    return (code_values.reshape(row_count, -1).astype(jnp.bfloat16), code_scale)


def decode_residual(code_values, code_scale, base_rows):
    row_count = code_values.shape[0]
    shaped = (
        code_values.astype(jnp.float32).reshape(row_count, -1, HD)
        * code_scale.astype(jnp.float32)[:, :, None]
    )
    return (base_rows.astype(jnp.float32) + shaped.reshape(row_count, -1)).astype(jnp.bfloat16)


def time_gate(step_value, w_time):
    half_feature_width = w_time.shape[0] // 2
    pair_index = jnp.arange(half_feature_width, dtype=jnp.float32)
    frequency = jnp.exp(-math.log(time_base) * pair_index / half_feature_width)
    phases = step_value.astype(jnp.float32) * frequency
    embedding = jnp.concatenate([jnp.cos(phases), jnp.sin(phases)])
    return jnp.sum(embedding[:, None] * w_time.astype(jnp.float32), axis=0)


def fold_update(fold_state, query_rows, key_piece, value_piece):
    running_max, running_sum, weighted = fold_state
    head_count = running_max.shape[0]
    score_scale = 1.0 / math.sqrt(HD)
    new_max, new_sum, new_weighted = ([], [], [])
    for head_index in range(head_count):
        lower = head_index * HD
        head_queries = query_rows[:, lower : lower + HD]
        head_keys = key_piece[:, lower : lower + HD]
        head_values = value_piece[:, lower : lower + HD]
        scores = (
            jnp.dot(head_queries, head_keys.T, preferred_element_type=jnp.float32) * score_scale
        )
        top_now = jnp.maximum(running_max[head_index], jnp.max(scores, axis=1))
        exponent = jnp.exp(scores - top_now[:, None])
        rescale = jnp.exp(running_max[head_index] - top_now)
        new_sum.append(running_sum[head_index] * rescale + jnp.sum(exponent, axis=1))
        mixed = jnp.dot(
            exponent.astype(jnp.bfloat16), head_values, preferred_element_type=jnp.float32
        )
        new_weighted.append(weighted[head_index] * rescale[:, None] + mixed)
        new_max.append(top_now)
    return (jnp.stack(new_max), jnp.stack(new_sum), jnp.stack(new_weighted))


def body(query_field, key_field, value_field, positions, timesteps, w_out, w_time):
    angles = band_angles(positions)
    cosine = jnp.cos(angles)
    sine_table = jnp.sin(angles)
    results = []
    own_keys = None
    own_values = None
    anchor_key_rows = None
    base_values = None
    for step_index in range(STEPS):
        rotated_q = rotate(query_field[step_index], cosine, sine_table)
        rotated_k = rotate(key_field[step_index], cosine, sine_table)
        fresh_values = value_field[step_index]
        query_rows, key_rows, value_rows = (
            lax.all_to_all(rotated_q, "head", split_axis=1, concat_axis=0, tiled=True),
            lax.all_to_all(rotated_k, "head", split_axis=1, concat_axis=0, tiled=True),
            lax.all_to_all(fresh_values, "head", split_axis=1, concat_axis=0, tiled=True),
        )
        head_count = query_rows.shape[1] // HD
        query_count = query_rows.shape[0]
        start_state = (
            jnp.full((head_count, query_count), lowest, jnp.float32),
            jnp.zeros((head_count, query_count), jnp.float32),
            jnp.zeros((head_count, query_count, HD), jnp.float32),
        )
        if step_index > 0:
            key_codes, key_scale = encode(key_rows, own_keys)
            value_codes, value_scale = encode(value_rows, own_values)
            own_keys = decode_residual(key_codes, key_scale, own_keys)
            own_values = decode_residual(value_codes, value_scale, own_values)
        if step_index == 0:
            anchor_key_rows, base_values = (
                lax.all_gather(key_rows, "seq", axis=0, tiled=True),
                lax.all_gather(value_rows, "seq", axis=0, tiled=True),
            )
            fold_state = fold_update(start_state, query_rows, anchor_key_rows, base_values)
        else:
            all_key_codes, all_value_codes, all_key_scales, all_value_scales = (
                lax.all_gather(key_codes, "seq", axis=0, tiled=True),
                lax.all_gather(value_codes, "seq", axis=0, tiled=True),
                lax.all_gather(key_scale, "seq", axis=0, tiled=True),
                lax.all_gather(value_scale, "seq", axis=0, tiled=True),
            )
            anchor_key_rows = decode_residual(all_key_codes, all_key_scales, anchor_key_rows)
            base_values = decode_residual(all_value_codes, all_value_scales, base_values)
            fold_state = fold_update(start_state, query_rows, anchor_key_rows, base_values)
        if step_index == 0:
            own_keys = key_rows
            own_values = value_rows
        running_max, running_sum, weighted = fold_state
        attended = (weighted / running_sum[:, :, None]).astype(jnp.bfloat16)
        attended = attended.transpose(1, 0, 2).reshape(query_count, head_count * HD)
        token_rows = lax.all_to_all(attended, "head", split_axis=0, concat_axis=1, tiled=True)
        partial_terms = jnp.dot(token_rows, w_out, preferred_element_type=jnp.float32)
        projected = lax.psum_scatter(partial_terms, "tp", scatter_dimension=1, tiled=True)
        gate_values = time_gate(timesteps[step_index], w_time)
        results.append((projected * gate_values[None, :]).astype(jnp.bfloat16))
    return jnp.stack(results)


MESH = pl.DeviceIdType.MESH


def feature_table():
    frame_band = HD // 8
    side_band = (HD - frame_band) // 2
    rope = []
    for band_width in (frame_band, side_band, side_band):
        pair_index = np.arange(band_width // 2)
        rope.append(np.repeat(rope_theta ** (-2.0 * pair_index / band_width), 2))
    table = np.zeros((8, HD), np.float32)
    table[0] = np.concatenate(rope)
    return table


def time_table(half_width):
    index = np.arange(half_width)
    table = np.zeros((8, half_width), np.float32)
    table[0] = np.exp(-math.log(time_base) * index / half_width)
    return table


def flipped(index, mask):
    out = index
    bit = 1
    while bit <= mask:
        if mask & bit:
            out = out + bit * (1 - 2 * ((index // bit) % 2))
        bit *= 2
    return out


def fused_kernel(
    sizes,
    q_hbm,
    k_hbm,
    v_hbm,
    pos_hbm,
    time_hbm,
    w_out_hbm,
    w_time_hbm,
    rope_hbm,
    freq_hbm,
    out_ref,
    q_in,
    k_in,
    v_in,
    pos_in,
    time_in,
    w_out,
    w_time,
    rope_in,
    freq_in,
    sent,
    got,
    att_out,
    att_in,
    part_out,
    part_in,
    part_own,
    gate_buf,
    load_sem,
    send_sem,
    recv_sem,
    att_send_sem,
    att_recv_sem,
    part_send_sem,
    part_recv_sem,
    ready_sem,
):
    n_seq, n_head, steps, tokens, half, chunk = sizes
    peers = n_seq * n_head
    chunks = half // chunk
    seq = lax.axis_index("seq")
    head = lax.axis_index("head")
    core = lax.axis_index("tp")
    me = seq * n_head + head

    loads = [
        pltpu.make_async_copy(source, target, load_sem.at[slot])
        for slot, (source, target) in enumerate(
            (
                (v_hbm, v_in),
                (pos_hbm, pos_in),
                (rope_hbm, rope_in),
                (k_hbm, k_in),
                (q_hbm, q_in),
                (time_hbm, time_in),
                (freq_hbm, freq_in),
                (w_time_hbm, w_time),
                (w_out_hbm, w_out),
            )
        )
    ]
    for load in loads:
        load.start()

    def place(mask):
        other = flipped(me, mask)
        return {"seq": other // n_head, "head": other % n_head}

    partner = {"tp": 1 - core}
    barrier = pltpu.get_barrier_semaphore()
    beside, along, mirror = 1, n_head, (n_seq - 1) * n_head
    staged = n_seq == 4 and n_head == 2
    greeted = (beside, along, mirror) if staged else range(1, peers)
    for mask in greeted:
        pl.semaphore_signal(barrier, inc=1, device_id=place(mask), device_id_type=MESH)
    pl.semaphore_signal(barrier, inc=1, device_id=partner, device_id_type=MESH)

    def tell(slot, mask):
        pl.semaphore_signal(
            ready_sem.at[slot], inc=1, device_id=place(mask), device_id_type=MESH
        )


    order = list(range(peers - 1, -1, -1))

    def columns(mask):
        return pl.ds(pl.multiple_of(flipped(me, mask) * HD, HD), HD)

    def rows(mask):
        return pl.ds(mask * tokens, tokens)

    def send(step, kind, mask):
        if kind == 2 and step == 0:
            source = v_in.at[0, :, columns(mask)]
        else:
            source = sent.at[step, kind, rows(mask)]
        return pltpu.make_async_remote_copy(
            src_ref=source,
            dst_ref=got.at[step, kind, rows(mask)],
            send_sem=send_sem.at[step, kind, mask],
            recv_sem=recv_sem.at[step, kind, mask],
            device_id=place(mask),
            device_id_type=MESH,
        )

    def emit(step, kind, mask, block):
        if mask == 0:
            got[step, kind, rows(0)] = block
        else:
            sent[step, kind, rows(mask)] = block
            send(step, kind, mask).start()

    loads[1].wait()
    loads[2].wait()
    place_row = pos_in[...].astype(jnp.float32)
    square = (tokens, tokens)
    diagonal = lax.broadcasted_iota(jnp.int32, square, 0) == lax.broadcasted_iota(
        jnp.int32, square, 1
    )
    place_column = jnp.sum(
        jnp.where(diagonal, jnp.broadcast_to(place_row, square), 0.0), axis=1, keepdims=True
    )
    plane = float(LAT_H * LAT_W)
    line = jnp.floor((place_column + 0.5) * (1.0 / LAT_W))
    frame_index = jnp.floor((place_column + 0.5) * (1.0 / plane))
    row_index = line - frame_index * LAT_H
    column_index = place_column - line * LAT_W
    lane = lax.broadcasted_iota(jnp.int32, (tokens, HD), 1)
    frame_band = HD // 8
    side_band = (HD - frame_band) // 2
    coordinate = jnp.where(
        lane < frame_band,
        frame_index,
        jnp.where(lane < frame_band + side_band, row_index, column_index),
    )
    angles = coordinate * rope_in[0:1, :]
    cosine = jnp.cos(angles)
    even = lane % 2 == 0
    sine = jnp.where(even, -jnp.sin(angles), jnp.sin(angles))

    def turned(block):
        wide = block.astype(jnp.float32)
        swapped = jnp.where(even, pltpu.roll(wide, HD - 1, 1), pltpu.roll(wide, 1, 1))
        return (wide * cosine + swapped * sine).astype(jnp.bfloat16)

    def recoded(fresh, base):
        wide_base = base.astype(jnp.float32)
        residual = fresh.astype(jnp.float32) - wide_base
        largest = jnp.max(jnp.abs(residual), axis=1, keepdims=True)
        scale = ((largest + 1e-06) / 120.0).astype(jnp.bfloat16).astype(jnp.float32)
        code = jnp.floor(residual / scale + 0.5)
        return (wide_base + code * scale).astype(jnp.bfloat16)

    loads[0].wait()
    pl.semaphore_wait(barrier, len(greeted) + 1)
    if staged:
        tell(0, beside)
        tell(1, along)
    far = order[: peers // 2]
    near = order[peers // 2 :]

    def emit_values(step, masks):
        for mask in masks:
            if step == 0 and mask == 0:
                got[0, 2, rows(0)] = v_in[0, :, columns(0)]
            elif step == 0:
                send(0, 2, mask).start()
            else:
                block = recoded(v_in[step, :, columns(mask)], v_in[step - 1, :, columns(mask)])
                if step + 1 < steps:
                    v_in[step, :, columns(mask)] = block
                emit(step, 2, mask, block)

    def emit_keys(step, masks):
        for mask in masks:
            block = turned(k_in[step, :, columns(mask)])
            if step > 0:
                kept = got if mask == 0 else sent
                block = recoded(block, kept[step - 1, 1, rows(mask)])
            emit(step, 1, mask, block)

    def emit_queries(step, masks):
        for mask in masks:
            emit(step, 0, mask, turned(q_in[step, :, columns(mask)]))

    if staged:
        far = [mirror, mirror + beside, mirror - along, mirror - along + beside]
    for turn, mask in enumerate(far):
        if staged and turn == 1:
            pl.semaphore_wait(ready_sem.at[0], 1)
        if staged and turn == 2:
            pl.semaphore_wait(ready_sem.at[1], 1)
            tell(2, beside)
        if staged and turn == 3:
            pl.semaphore_wait(ready_sem.at[2], 1)
        emit_values(0, [mask])
        if turn == 0:
            loads[3].wait()
        emit_keys(0, [mask])
        if turn == 0:
            loads[4].wait()
        emit_queries(0, [mask])
        if turn == 0 and staged and steps > 1:
            emit_values(1, [mask])
            emit_keys(1, [mask])
    emit_values(0, near)
    emit_keys(0, near)
    emit_queries(0, near)
    for step in range(1, steps):
        late = far[1:] if staged and step == 1 else far
        emit_values(step, late)
        emit_keys(step, late)
        emit_values(step, near)
        emit_keys(step, near)
        emit_queries(step, near)
        emit_queries(step, far)

    for load in loads[5:8]:
        load.wait()
    half_width = freq_in.shape[1]
    for step in range(steps):
        phases = time_in[0:1, step : step + 1].astype(jnp.float32) * freq_in[0:1, :]
        total = jnp.zeros((8, half), jnp.float32)
        for lower, wave in ((0, jnp.cos(phases)), (half_width, jnp.sin(phases))):
            first = wave.astype(jnp.bfloat16)
            rest = wave - first.astype(jnp.float32)
            second = rest.astype(jnp.bfloat16)
            third = (rest - second.astype(jnp.float32)).astype(jnp.bfloat16)
            which = lax.broadcasted_iota(jnp.int32, (8, half_width), 0)
            stacked = jnp.where(
                which == 0,
                first.astype(jnp.float32),
                jnp.where(
                    which == 1,
                    second.astype(jnp.float32),
                    jnp.where(which == 2, third.astype(jnp.float32), 0.0),
                ),
            ).astype(jnp.bfloat16)
            total = total + jnp.dot(
                stacked, w_time[lower : lower + half_width, :], preferred_element_type=jnp.float32
            )
        gate_buf[step] = jnp.broadcast_to(jnp.sum(total, axis=0, keepdims=True), (8, half))

    def give_back(step, mask):
        return pltpu.make_async_remote_copy(
            src_ref=att_out.at[step, rows(mask)],
            dst_ref=att_in.at[step, :, columns(0)],
            send_sem=att_send_sem.at[step, mask],
            recv_sem=att_recv_sem.at[step, mask],
            device_id=place(mask),
            device_id_type=MESH,
        )

    score_scale = 1.0 / math.sqrt(HD)

    def attend(step):
        for kind in (2, 1):
            for mask in range(1, peers):
                send(step, kind, mask).wait_recv()
        keys = got[step, 1]
        values = got[step, 2]
        for start, count in ((0, peers // 2), (peers // 2, peers // 2)):
            for mask in range(start, start + count):
                if mask > 0:
                    send(step, 0, mask).wait_recv()
            queries = got[step, 0, start * tokens : (start + count) * tokens]
            scores = (
                lax.dot_general(
                    queries, keys, (((1,), (1,)), ((), ())), preferred_element_type=jnp.float32
                )
                * score_scale
            )
            weights = jnp.exp(scores - jnp.max(scores, axis=1, keepdims=True))
            totals = jnp.sum(weights, axis=1, keepdims=True)
            mixed = jnp.dot(
                weights.astype(jnp.bfloat16), values, preferred_element_type=jnp.float32
            )
            attended = (mixed / totals).astype(jnp.bfloat16)
            for mask in range(start, start + count):
                block = attended[(mask - start) * tokens : (mask - start + 1) * tokens]
                if mask == 0:
                    att_in[step, :, columns(0)] = block
                else:
                    att_out[step, rows(mask)] = block
                    give_back(step, mask).start()

    def share(step, piece):
        return pltpu.make_async_remote_copy(
            src_ref=part_out.at[step, piece],
            dst_ref=part_in.at[step, piece],
            send_sem=part_send_sem.at[step, piece],
            recv_sem=part_recv_sem.at[step, piece],
            device_id=partner,
            device_id_type=MESH,
        )

    def project(step):
        depth = att_in.shape[2] // 2
        side = seq // (n_seq // 2)
        if step == 0:
            loads[8].wait()
        for masks, block in ((range(1, peers // 2), side), (range(peers // 2, peers), 1 - side)):
            for mask in masks:
                pltpu.make_async_remote_copy(
                    src_ref=att_out.at[step, rows(mask)],
                    dst_ref=att_in.at[step, :, columns(mask)],
                    send_sem=att_send_sem.at[step, mask],
                    recv_sem=att_recv_sem.at[step, mask],
                    device_id=place(mask),
                    device_id_type=MESH,
                ).wait_recv()
            features = pl.ds(pl.multiple_of(block * depth, depth), depth)
            attended = att_in[step, :, features]
            first = masks[0] == 1
            for target, part in ((1 - core, part_out), (core, part_own)):
                for piece in range(chunks):
                    lower = pl.multiple_of(target * half + piece * chunk, HD)
                    term = jnp.dot(
                        attended,
                        w_out[features, pl.ds(lower, chunk)],
                        preferred_element_type=jnp.float32,
                    )
                    part[step, piece] = (term if first else part[step, piece] + term).astype(part.dtype)
                    if part is part_out and not first:
                        share(step, piece).start()

    def finish(step):
        for piece in range(chunks):
            share(step, piece).wait_recv()
            cut = slice(piece * chunk, (piece + 1) * chunk)
            projected = part_own[step, piece] + part_in[step, piece]
            out_ref[step, :, cut] = (projected * gate_buf[step, 0:1, cut]).astype(jnp.bfloat16)

    for step in range(steps):
        attend(step)
    for step in range(steps):
        project(step)
        if step > 0:
            finish(step - 1)
    finish(steps - 1)

    for step in range(steps):
        for mask in range(1, peers):
            for kind in range(3):
                send(step, kind, mask).wait_send()
            give_back(step, mask).wait_send()
        for piece in range(chunks):
            share(step, piece).wait_send()


def fused_body(n_seq, n_head, query_field, key_field, value_field, positions, timesteps, w_out, w_time):
    steps, tokens, features = query_field.shape
    half = w_time.shape[1]
    peers = n_seq * n_head
    chunk = 512 if half % 512 == 0 else HD
    chunks = half // chunk
    bf16, f32 = jnp.bfloat16, jnp.float32
    dma = pltpu.SemaphoreType.DMA
    rope = jnp.asarray(feature_table())
    freq = jnp.asarray(time_table(w_time.shape[0] // 2))
    sizes = (n_seq, n_head, steps, tokens, half, chunk)
    scratch = [
        pltpu.VMEM(query_field.shape, bf16),
        pltpu.VMEM(key_field.shape, bf16),
        pltpu.VMEM(value_field.shape, bf16),
        pltpu.VMEM((1, tokens), jnp.int32),
        pltpu.VMEM((1, steps), jnp.int32),
        pltpu.VMEM(w_out.shape, bf16),
        pltpu.VMEM(w_time.shape, bf16),
        pltpu.VMEM(rope.shape, f32),
        pltpu.VMEM(freq.shape, f32),
        pltpu.VMEM((steps, 3, peers * tokens, HD), bf16),
        pltpu.VMEM((steps, 3, peers * tokens, HD), bf16),
        pltpu.VMEM((steps, peers * tokens, HD), bf16),
        pltpu.VMEM((steps, tokens, features), bf16),
        pltpu.VMEM((steps, chunks, tokens, chunk), bf16),
        pltpu.VMEM((steps, chunks, tokens, chunk), bf16),
        pltpu.VMEM((steps, chunks, tokens, chunk), f32),
        pltpu.VMEM((steps, 8, half), f32),
        dma((9,)),
        dma((steps, 3, peers)),
        dma((steps, 3, peers)),
        dma((steps, peers)),
        dma((steps, peers)),
        dma((steps, chunks)),
        dma((steps, chunks)),
        pltpu.SemaphoreType.REGULAR((3,)),
    ]
    return pl.pallas_call(
        lambda *refs: fused_kernel(sizes, *refs),
        out_shape=pltpu.VMEM((steps, tokens, half), bf16),
        in_specs=[pl.BlockSpec(memory_space=pltpu.HBM)] * 9,
        out_specs=pl.BlockSpec(memory_space=pltpu.VMEM),
        scratch_shapes=scratch,
        compiler_params=pltpu.CompilerParams(
            collective_id=0, has_side_effects=True, vmem_limit_bytes=56 * 1024 * 1024
        ),
    )(
        query_field,
        key_field,
        value_field,
        positions.reshape(1, tokens),
        timesteps.reshape(1, steps),
        w_out,
        w_time,
        rope,
        freq,
    )


def solution(mesh):
    placed = (
        P(None, ("group", "seq", "head"), "tp"),
        P(None, ("group", "seq", "head"), "tp"),
        P(None, ("group", "seq", "head"), "tp"),
        P(("group", "seq", "head")),
        P("group"),
        P("tp", None),
        P(None, "tp"),
    )
    n_seq, n_head = mesh.shape["seq"], mesh.shape["head"]
    peers = n_seq * n_head

    def chosen(query_field, *rest):
        local_heads = query_field.shape[2] // HD
        tokens = query_field.shape[1]
        if (
            local_heads == peers
            and peers & (peers - 1) == 0
            and peers >= 4
            and n_seq % 2 == 0
            and mesh.shape["tp"] == 2
            and tokens % 16 == 0
        ):
            return fused_body(n_seq, n_head, query_field, *rest)
        return body(query_field, *rest)

    return jax.shard_map(
        chosen,
        mesh=mesh,
        in_specs=placed,
        out_specs=P(None, ("group", "seq", "head"), "tp"),
        check_vma=False,
    )
```
